256 devices in a mesh: coil: 16 (over y, x_lo, core), slab: 16 (over z, x_hi).
Axes of the slice: x: 4 (x_hi: 2, x_lo: 2; x = x_hi * 2 + x_lo), y: 4, z: 8, core: 2. Of those that a mesh axis runs over, the one named last changes fastest.
Arguments:
- estimate: float32 [2, 128, 128, 128], P(None, 'slab', 'coil'), may hold values from -6 to 6
- coil_maps: float32 [32, 2, 128, 128, 128], P('coil', None, 'slab'), may hold values from -2 to 2
- measured: float32 [32, 2, 128, 128, 128], P('coil', None, None, 'slab'), may hold values from -3 to 3
- line_mask: int32 [128, 128], replicated, may hold values 0 or 1
- w_first: float32 [27, 32, 2], replicated, may hold values from -0.875 to 0.875
- w_middle: float32 [27, 32, 32], replicated, may hold values from -0.21875 to 0.21875
- w_last: float32 [27, 2, 32], replicated, may hold values from -0.21875 to 0.21875
Outputs:
- combined: float32 [2, 128, 128, 128], P(None, 'slab', 'coil')
- refined: float32 [2, 128, 128, 128], P(None, 'slab', 'coil')
The draws below stay inside these ranges and needn't reach their ends.
Inputs may be any that keep to these rules, and one draw needn't show every extreme that they name: `line_mask`: 1 marks a sampled line.
All inputs are finite; a program needn't handle non-finite values.
Results may differ from the reference program's by a relative error of at most 0.0001.
Values sent between devices are 32-bit elements; how exact they have to be, the bound alone decides.
A program may use at most 192 MiB of HBM per device.

```python
import jax
import jax.numpy as jnp
from jax import lax

NZ = 128
NX = 128
NY = 128
CH = 32
COILS = 32


def place_ends(drawn, key, least, top_value):
    spot = [jax.random.randint(jax.random.fold_in(key, axis), (), 0, length) for axis, length in enumerate(drawn.shape)]
    main_axis = drawn.shape.index(max(drawn.shape))
    beside = spot[:main_axis] + [(spot[main_axis] + 1) % drawn.shape[main_axis]] + spot[main_axis + 1:]
    return drawn.at[tuple(spot)].set(least).at[tuple(beside)].set(top_value)


def levels(rng, dims, cuts, least, high):
    def one(axis_at, blocks):
        draws = jax.random.uniform(jax.random.fold_in(jax.random.fold_in(rng, 6), axis_at), (blocks,), jnp.float32, least / len(cuts), high / len(cuts))
        return jnp.repeat(jnp.exp(draws), dims[axis_at] // blocks).reshape((-1,) + (1,) * (len(dims) - axis_at - 1))

    factor_of = one(*cuts[0])
    for cut in cuts[1:]:
        factor_of = factor_of * one(*cut)
    return factor_of


def centred(stream_key, dims, scale, limit, cuts=(), kind=jnp.bfloat16):
    loudness = levels(stream_key, dims, cuts, -0.22, 0.18) if cuts else 1.0
    drawn = jax.random.normal(stream_key, dims, jnp.float32) * scale * loudness
    return jnp.minimum(jnp.maximum(drawn, -limit), limit).astype(kind)


def setup_inputs(seed: int = 0) -> dict:
    seeds = jax.random.split(jax.random.key(seed), 8)
    estimate = centred(seeds[0], (2, NZ, NX, NY), 1.0, 6.0, ((1, 16), (2, 16)), jnp.float32)
    coil_maps = centred(seeds[1], (COILS, 2, NZ, NX, NY), ((2 * COILS) ** -0.5), 2.0, ((0, 16), (2, 16)), jnp.float32)
    measured = centred(seeds[2], (COILS, 2, NZ, NX, NY), 0.2, 3.0, ((0, 16), (3, 16)), jnp.float32)
    line_mask = place_ends((jax.random.randint(seeds[3], (NZ, NY), 0, 3) < 1).astype(jnp.int32), jax.random.fold_in(seeds[3], 1), 0, 1)
    w_first = centred(seeds[4], (27, CH, 2), 54 ** -0.5, 0.875, (), jnp.float32)
    w_middle = centred(seeds[5], (27, CH, CH), (27 * CH) ** -0.5, 0.21875, (), jnp.float32)
    w_last = centred(seeds[6], (27, 2, CH), (27 * CH) ** -0.5, 0.21875, (), jnp.float32)
    return {"estimate": estimate, "coil_maps": coil_maps, "measured": measured, "line_mask": line_mask, "w_first": w_first, "w_middle": w_middle, "w_last": w_last}


def conv_layer(field, weights):
    kernel = jnp.transpose(weights.reshape(3, 3, 3, weights.shape[1], weights.shape[2]), (3, 4, 0, 1, 2))
    output = lax.conv_general_dilated(field[None], kernel, (1, 1, 1), [(1, 1), (1, 1), (1, 1)],
                                      dimension_numbers=("NCDHW", "OIDHW", "NCDHW"),
                                      precision=lax.Precision.HIGHEST)
    return output[0]


def reference(estimate, coil_maps, measured, line_mask, w_first, w_middle, w_last):
    image_real = estimate[0]
    image_imag = estimate[1]
    weighting = (line_mask == 1).astype(jnp.float32)[:, None, :] * 0.5

    def one_coil(carry, items):
        map_real, map_imag, data_real, data_imag = items
        coil_image = (map_real * image_real - map_imag * image_imag) + 1j * (map_real * image_imag + map_imag * image_real)
        spectrum = jnp.fft.fftn(coil_image, norm="ortho")
        spectrum = spectrum - weighting * (spectrum - (data_real + 1j * data_imag))
        back = jnp.fft.ifftn(spectrum, norm="ortho")
        total_real = carry[0] + map_real * back.real + map_imag * back.imag
        total_imag = carry[1] + map_real * back.imag - map_imag * back.real
        return (total_real, total_imag), None

    start = (jnp.zeros_like(image_real), jnp.zeros_like(image_real))
    totals, unused = lax.scan(one_coil, start, (coil_maps[:, 0], coil_maps[:, 1], measured[:, 0], measured[:, 1]))
    combined = jnp.stack([totals[0], totals[1]])
    hidden = jax.nn.relu(conv_layer(combined, w_first))
    hidden = jax.nn.relu(conv_layer(hidden, w_middle))
    refined = combined + conv_layer(hidden, w_last)
    return combined, refined
```

```python
import math

import jax
import jax.numpy as jnp
import ml_dtypes
import numpy as np
from jax import lax
from jax.experimental import pallas as pl
from jax.experimental.pallas import tpu as pltpu
from jax.sharding import PartitionSpec as P

MESH = pl.DeviceIdType.MESH
F32 = jnp.float32
BF16 = jnp.bfloat16
N = 128
B = 8
G = 16


def tables():
    k = np.arange(N)
    angle = 2.0 * math.pi * (np.outer(k, k) % N) / N
    c, s = np.cos(angle) / math.sqrt(N), np.sin(angle) / math.sqrt(N)
    fwd = np.block([[c, s], [-s, c]])
    inv = np.block([[c, -s], [s, c]])

    def pieces(m):
        hi = m.astype(np.float32).astype(ml_dtypes.bfloat16)
        lo = (m - hi.astype(np.float64)).astype(np.float32).astype(ml_dtypes.bfloat16)
        return [hi, hi, lo]

    return [
        np.concatenate(pieces(fwd), 1),
        np.concatenate(pieces(inv), 1),
        np.concatenate(pieces(inv), 0),
        np.concatenate(pieces(fwd), 0),
    ]


def split(x):
    hi = x.astype(BF16)
    lo = (x - hi.astype(F32)).astype(BF16)
    return hi, lo


def left(table, x):
    hi, lo = split(x)
    return jnp.dot(table, jnp.concatenate([hi, lo, hi], 0), preferred_element_type=F32)


def right(x, table):
    hi, lo = split(x)
    return jnp.dot(jnp.concatenate([hi, lo, hi], 1), table, preferred_element_type=F32)


def loop(count, fn):
    def step(i, carry):
        fn(i)
        return carry

    lax.fori_loop(0, count, step, 0)


def recon_kernel(
    est, maps, meas, weight, lf, li, rf, ri_,
    out,
    gath, send1, recv1, send2, recv2, part, rs_a, rs_b,
    ag_send, ag_recv, a1_send, a1_recv, a2_send, a2_recv, own_sem, rs_send, rs_recv,
):
    me_c = lax.axis_index("coil")
    me_s = lax.axis_index("slab")
    core = lax.rem(me_c, 2)
    chip = me_c // 2
    sibling = me_c + 1 - 2 * core

    barrier = pltpu.get_barrier_semaphore()

    def greet(k):
        pl.semaphore_signal(barrier, inc=1, device_id={"coil": lax.rem(me_c + k + 1, G)}, device_id_type=MESH)
        pl.semaphore_signal(barrier, inc=1, device_id={"slab": lax.rem(me_s + k + 1, G)}, device_id_type=MESH)

    loop(G - 1, greet)
    pl.semaphore_wait(barrier, 2 * (G - 1))

    def ag_copy(src, slot, send_i, target):
        return pltpu.make_async_remote_copy(
            src_ref=src, dst_ref=gath.at[slot], send_sem=ag_send.at[send_i], recv_sem=ag_recv.at[slot],
            device_id={"coil": target}, device_id_type=MESH)

    ag_copy(est, me_c, 0, sibling).start()

    def ag_out(k):
        ag_copy(est, me_c, 1 + k, 2 * lax.rem(chip + k + 1, 8) + core).start()

    loop(7, ag_out)
    gath[me_c] = est[...]

    def ag_in(k):
        slot = 2 * lax.rem(chip + 7 - k, 8) + core
        ag_copy(est, slot, 0, sibling).wait_recv()
        ag_copy(gath.at[slot], slot, 8 + k, sibling).start()

    loop(7, ag_in)

    def ag_last(k):
        slot = 2 * lax.rem(chip + 8 - k, 8) + 1 - core
        ag_copy(est, slot, 0, sibling).wait_recv()

    loop(8, ag_last)

    def a1_copy(c, h, peer, slot):
        return pltpu.make_async_remote_copy(
            src_ref=send1.at[c, :, pl.ds(pl.multiple_of(peer * 64 + h * 32, 32), 32), :],
            dst_ref=recv1.at[c, h, slot],
            send_sem=a1_send.at[2 * c + h, peer], recv_sem=a1_recv.at[2 * c + h, slot],
            device_id={"slab": peer}, device_id_type=MESH)

    def a1_own(c, h):
        return pltpu.make_async_copy(
            send1.at[c, :, pl.ds(pl.multiple_of(me_s * 64 + h * 32, 32), 32), :],
            recv1.at[c, h, me_s], own_sem.at[2 * c + h])

    for c in range(2):
        def fx(zp):
            cols = []
            for j in range(2):
                z = 2 * zp + j
                ir = gath[:, 0, z].reshape(N, N)
                ii = gath[:, 1, z].reshape(N, N)
                mr = maps[c, 0, z]
                mi = maps[c, 1, z]
                cols.append(jnp.concatenate([mr * ir - mi * ii, mr * ii + mi * ir], 0))
            y = left(lf[...], jnp.concatenate(cols, 1))
            for j in range(2):
                for r in range(2):
                    send1[c, r, pl.ds(2 * zp + j, N, stride=B), :] = y[r * N:(r + 1) * N, j * N:(j + 1) * N]

        loop(4, fx)
        for h in range(2):
            def a1_out(k):
                peer = lax.rem(me_s + k + 1, G)
                a1_copy(c, h, peer, me_s).start()

            loop(G - 1, a1_out)
            a1_own(c, h).start()

    def a2_copy(c, h, peer, slot):
        return pltpu.make_async_remote_copy(
            src_ref=send2.at[c, h, peer],
            dst_ref=recv2.at[c, :, pl.ds(pl.multiple_of(slot * 64 + h * 32, 32), 32), :],
            send_sem=a2_send.at[2 * c + h, peer], recv_sem=a2_recv.at[2 * c + h, slot],
            device_id={"slab": peer}, device_id_type=MESH)

    def a2_own(c, h):
        return pltpu.make_async_copy(
            send2.at[c, h, me_s],
            recv2.at[c, :, pl.ds(pl.multiple_of(me_s * 64 + h * 32, 32), 32), :], own_sem.at[4 + 2 * c + h])

    def pencil_chunk(q):
        c = q // 2
        h = lax.rem(q, 2)

        def a1_in(k):
            peer = lax.rem(me_s + G - 1 - k, G)
            a1_copy(c, h, me_s, peer).wait_recv()

        a1_own(c, h).wait()
        loop(G - 1, a1_in)

        def pair(kp):
            rows = []
            for j in range(2):
                at = pl.ds(pl.multiple_of((2 * kp + j) * B, B), B)
                rows.append(jnp.concatenate(
                    [recv1[c, h, :, 0, at, :].reshape(N, N), recv1[c, h, :, 1, at, :].reshape(N, N)], 1))
            y = right(jnp.concatenate(rows, 0), rf[...])
            x = jnp.concatenate([
                jnp.concatenate([y[:N, :N], y[N:, :N]], 1),
                jnp.concatenate([y[:N, N:], y[N:, N:]], 1)], 0)
            x = left(lf[...], x)
            w = weight[...]
            halves = []
            for r in range(2):
                pieces = []
                for j in range(2):
                    k = x[r * N:(r + 1) * N, j * N:(j + 1) * N]
                    m = meas[c, r, pl.ds(h * 4 + 2 * kp + j, N, stride=B), :]
                    pieces.append(k - w * (k - m))
                halves.append(jnp.concatenate(pieces, 1))
            x = left(li[...], jnp.concatenate(halves, 0))
            y = jnp.concatenate([
                jnp.concatenate([x[:N, :N], x[N:, :N]], 1),
                jnp.concatenate([x[:N, N:], x[N:, N:]], 1)], 0)
            y = right(y, ri_[...])
            for j in range(2):
                for r in range(2):
                    send2[c, h, :, r, pl.ds(pl.multiple_of((2 * kp + j) * B, B), B), :] = (
                        y[j * N:(j + 1) * N, r * N:(r + 1) * N].reshape(G, B, N))

        loop(2, pair)

        def a2_out(k):
            peer = lax.rem(me_s + k + 1, G)
            a2_copy(c, h, peer, me_s).start()

        loop(G - 1, a2_out)
        a2_own(c, h).start()

    loop(4, pencil_chunk)

    for c in range(2):
        for h in range(2):
            def a2_in(k):
                peer = lax.rem(me_s + G - 1 - k, G)
                a2_copy(c, h, me_s, peer).wait_recv()

            a2_own(c, h).wait()
            loop(G - 1, a2_in)

        def fx_back(zp):
            cols = []
            for j in range(2):
                at = pl.ds(2 * zp + j, N, stride=B)
                cols.append(jnp.concatenate([recv2[c, 0, at, :], recv2[c, 1, at, :]], 0))
            x = left(li[...], jnp.concatenate(cols, 1))
            for j in range(2):
                z = 2 * zp + j
                br = x[:N, j * N:(j + 1) * N]
                bi = x[N:, j * N:(j + 1) * N]
                mr = maps[c, 0, z]
                mi = maps[c, 1, z]
                pr = (mr * br + mi * bi).reshape(8, 2, B, N)
                pi = (mr * bi - mi * br).reshape(8, 2, B, N)
                for g in range(2):
                    if c == 0:
                        part[g, :, 0, z] = pr[:, g]
                        part[g, :, 1, z] = pi[:, g]
                    else:
                        part[g, :, 0, z] = part[g, :, 0, z] + pr[:, g]
                        part[g, :, 1, z] = part[g, :, 1, z] + pi[:, g]

        loop(4, fx_back)

    to_sibling = pltpu.make_async_remote_copy(
        src_ref=part.at[1 - core], dst_ref=rs_a, send_sem=rs_send.at[8], recv_sem=rs_recv.at[8],
        device_id={"coil": sibling}, device_id_type=MESH)
    to_sibling.start()
    to_sibling.wait_recv()

    def rs_copy(target, slot):
        return pltpu.make_async_remote_copy(
            src_ref=rs_a.at[target], dst_ref=rs_b.at[slot], send_sem=rs_send.at[target], recv_sem=rs_recv.at[slot],
            device_id={"coil": 2 * target + core}, device_id_type=MESH)

    def rs_out(k):
        target = lax.rem(chip + k + 1, 8)
        rs_a[target] = rs_a[target] + part[core, target]
        rs_copy(target, chip).start()

    loop(7, rs_out)
    out[...] = rs_a[chip] + part[core, chip]

    def rs_in(k):
        slot = lax.rem(chip + 7 - k, 8)
        rs_copy(chip, slot).wait_recv()
        out[...] = out[...] + rs_b[slot]

    loop(7, rs_in)

    to_sibling.wait_send()

    def drain_small(k):
        rs_copy(lax.rem(chip + k + 1, 8), chip).wait_send()

    loop(7, drain_small)

    def drain_ag(k):
        ag_copy(est, me_c, k, sibling).wait_send()

    loop(15, drain_ag)

    def drain_a2a(i):
        q = i // (G - 1)
        peer = lax.rem(me_s + lax.rem(i, G - 1) + 1, G)
        a1_copy(q // 2, lax.rem(q, 2), peer, me_s).wait_send()
        a2_copy(q // 2, lax.rem(q, 2), peer, me_s).wait_send()

    loop(4 * (G - 1), drain_a2a)


def recon(estimate, coil_maps, measured, weight, tabs):
    measured = measured.reshape(2, 2, N * B, N)
    vmem = pl.BlockSpec(memory_space=pltpu.VMEM)
    dma = pltpu.SemaphoreType.DMA
    return pl.pallas_call(
        recon_kernel,
        out_shape=jax.ShapeDtypeStruct((2, B, B, N), F32),
        in_specs=[vmem] * 8,
        out_specs=vmem,
        scratch_shapes=[
            pltpu.VMEM((G, 2, B, B, N), F32),
            pltpu.VMEM((2, 2, N * B, N), F32),
            pltpu.VMEM((2, 2, G, 2, 32, N), F32),
            pltpu.VMEM((2, 2, G, 2, 32, N), F32),
            pltpu.VMEM((2, 2, N * B, N), F32),
            pltpu.VMEM((2, 8, 2, B, B, N), F32),
            pltpu.VMEM((8, 2, B, B, N), F32),
            pltpu.VMEM((8, 2, B, B, N), F32),
            dma((15,)), dma((G,)), dma((4, G)), dma((4, G)), dma((4, G)), dma((4, G)), dma((8,)), dma((9,)), dma((9,)),
        ],
        compiler_params=pltpu.CompilerParams(
            collective_id=0, has_side_effects=True, vmem_limit_bytes=48 * 2**20),
    )(estimate, coil_maps, measured, weight, *tabs)


def conv_weights(w_first, w_middle, w_last):
    def select(outs, ins, shift):
        x, d, i = np.ogrid[:outs, :3, :ins]
        return jnp.asarray((i - shift == x + d).astype(np.float32))

    def pieces(w, axis):
        hi = lax.reduce_precision(w, 8, 7)
        return jnp.stack([hi, hi, w - hi], axis).astype(BF16)

    hp = lax.Precision.HIGHEST
    w1 = jnp.einsum("zxyoc,pxq->ypozcq", w_first.reshape(3, 3, 3, 32, 2), select(12, 24, 5), precision=hp)
    w1 = pieces(w1.reshape(1152, 3, 48), 2).reshape(1152, 432)
    w2 = jnp.einsum("zxyoc,pxq->ypozqc", w_middle.reshape(3, 3, 3, 32, 32), select(5, 8, 0), precision=hp)
    w2 = pieces(w2.reshape(480, 3, 256), 2).reshape(480, 2304)
    w3 = jnp.einsum("zxyoc,pxq->zyopqc", w_last.reshape(3, 3, 3, 2, 32), select(8, 10, 0), precision=hp)
    w3 = pieces(w3.reshape(144, 320), 1).reshape(144, 960)
    return w1, w2, w3


def shifted_sum(p0, p1, p2):
    lane = lax.broadcasted_iota(jnp.int32, p0.shape, 1)
    down = jnp.where(lane == 0, 0.0, pltpu.roll(p0, 1, 1))
    up = jnp.where(lane == N - 1, 0.0, pltpu.roll(p2, N - 1, 1))
    return p1 + down + up


def denoise_kernel(comb, w1, w2, w3, refined, big, f0h, f0l, f1h, f1l, f2h, f2l, q3, send_sem, recv_sem):
    me_c = lax.axis_index("coil")
    me_s = lax.axis_index("slab")
    barrier = pltpu.get_barrier_semaphore()
    near = [(a, b) for a in (-1, 0, 1) for b in (-1, 0, 1) if (a, b) != (0, 0)]

    def target(dz, dx):
        return {"coil": lax.rem(me_c + dx + G, G), "slab": lax.rem(me_s + dz + G, G)}

    for dz, dx in near:
        pl.semaphore_signal(barrier, inc=1, device_id=target(dz, dx), device_id_type=MESH)
    pl.semaphore_wait(barrier, 8)

    source = {-1: (0, 3), 0: (0, 8), 1: (5, 3)}
    place = {-1: (11, 3), 0: (3, 8), 1: (0, 3)}
    copies = []
    for i, (dz, dx) in enumerate(near):
        a, n = source[dz]
        b, n = place[dz]
        copies.append(pltpu.make_async_remote_copy(
            src_ref=comb.at[:, pl.ds(a, n)], dst_ref=big.at[1 - dx, :, pl.ds(b, n)],
            send_sem=send_sem.at[i], recv_sem=recv_sem.at[i],
            device_id=target(dz, dx), device_id_type=MESH))
        copies[-1].start()
    big[1, :, 3:11] = comb[...]
    f1h[384:, :] = jnp.zeros((32, 12 * N), BF16)
    f1l[384:, :] = jnp.zeros((32, 12 * N), BF16)
    for copy in copies:
        copy.wait_recv()

    for z in range(14):
        rows = []
        for c in range(2):
            for blk in range(3):
                v = big[blk, c, z]
                if blk == 0:
                    v = jnp.where(me_c == 0, 0.0, v)
                if blk == 2:
                    v = jnp.where(me_c == G - 1, 0.0, v)
                if z < 3:
                    v = jnp.where(me_s == 0, 0.0, v)
                if z >= 11:
                    v = jnp.where(me_s == G - 1, 0.0, v)
                rows.append(v)
        hi, lo = split(jnp.concatenate(rows, 0))
        f0h[:, z * N:(z + 1) * N] = hi
        f0l[:, z * N:(z + 1) * N] = lo

    def inside(rows, first_x, z):
        x = me_c * B + first_x + lax.broadcasted_iota(jnp.int32, (rows, N), 0) // 32
        z = me_s * B + z
        return (x >= 0) & (x < N) & (z >= 0) & (z < N)

    def conv1(i):
        parts = []
        for dz in range(3):
            at = pl.ds(pl.multiple_of((2 * i + dz) * N, N), 2 * N)
            hi = f0h[:, at]
            parts += [hi, f0l[:, at], hi]
        y = jnp.dot(w1[...], jnp.concatenate(parts, 0), preferred_element_type=F32)
        for j in range(2):
            p = [y[d * 384:(d + 1) * 384, j * N:(j + 1) * N] for d in range(3)]
            v = jnp.maximum(shifted_sum(*p), 0.0)
            v = jnp.where(inside(384, -2, 2 * i + j - 2), v, 0.0)
            hi, lo = split(v)
            at = pl.ds(pl.multiple_of((2 * i + j) * N, N), N)
            f1h[0:384, at] = hi
            f1l[0:384, at] = lo

    loop(6, conv1)

    def conv2(i):
        for g in range(2):
            parts = []
            for dz in range(3):
                at = pl.ds(pl.multiple_of((2 * i + dz) * N, N), 2 * N)
                hi = f1h[g * 160:g * 160 + 256, at]
                parts += [hi, f1l[g * 160:g * 160 + 256, at], hi]
            y = jnp.dot(w2[...], jnp.concatenate(parts, 0), preferred_element_type=F32)
            for j in range(2):
                p = [y[d * 160:(d + 1) * 160, j * N:(j + 1) * N] for d in range(3)]
                v = jnp.maximum(shifted_sum(*p), 0.0)
                v = jnp.where(inside(160, g * 5 - 1, 2 * i + j - 1), v, 0.0)
                hi, lo = split(v)
                at = pl.ds(pl.multiple_of((2 * i + j) * N, N), N)
                f2h[g * 160:(g + 1) * 160, at] = hi
                f2l[g * 160:(g + 1) * 160, at] = lo

    loop(5, conv2)

    def conv3(i):
        at = pl.ds(pl.multiple_of(2 * i * N, N), 2 * N)
        hi = f2h[:, at]
        y = jnp.dot(w3[...], jnp.concatenate([hi, f2l[:, at], hi], 0), preferred_element_type=F32)
        q3[2 * i] = y[:, :N]
        q3[2 * i + 1] = y[:, N:]

    loop(5, conv3)

    def last(z):
        p = []
        for dy in range(3):
            p.append(sum(q3[z + dz, dz * 48 + dy * 16:dz * 48 + dy * 16 + 16, :] for dz in range(3)))
        v = shifted_sum(*p)
        refined[0, z] = comb[0, z] + v[:B]
        refined[1, z] = comb[1, z] + v[B:]

    loop(B, last)
    for copy in copies:
        copy.wait_send()


def denoise(combined, w1, w2, w3):
    vmem = pl.BlockSpec(memory_space=pltpu.VMEM)
    dma = pltpu.SemaphoreType.DMA
    return pl.pallas_call(
        denoise_kernel,
        out_shape=jax.ShapeDtypeStruct((2, B, B, N), F32),
        in_specs=[vmem] * 4,
        out_specs=vmem,
        scratch_shapes=[
            pltpu.VMEM((3, 2, 14, B, N), F32),
            pltpu.VMEM((48, 14 * N), BF16), pltpu.VMEM((48, 14 * N), BF16),
            pltpu.VMEM((416, 12 * N), BF16), pltpu.VMEM((416, 12 * N), BF16),
            pltpu.VMEM((320, 10 * N), BF16), pltpu.VMEM((320, 10 * N), BF16),
            pltpu.VMEM((10, 144, N), F32),
            dma((8,)), dma((8,)),
        ],
        compiler_params=pltpu.CompilerParams(
            collective_id=1, has_side_effects=True, vmem_limit_bytes=48 * 2**20),
    )(combined, w1, w2, w3)


def body(estimate, coil_maps, measured, line_mask, w_first, w_middle, w_last):
    tabs = [jnp.asarray(t) for t in tables()]
    weight = (line_mask == 1).astype(F32) * 0.5
    combined = recon(estimate, coil_maps, measured, weight, tabs)
    refined = denoise(combined, *conv_weights(w_first, w_middle, w_last))
    return combined, refined


def solution(mesh):
    in_specs = (
        P(None, "slab", "coil", None),
        P("coil", None, "slab", None, None),
        P("coil", None, None, "slab", None),
        P(),
        P(),
        P(),
        P(),
    )
    out_specs = (P(None, "slab", "coil", None), P(None, "slab", "coil", None))
    return jax.shard_map(body, mesh=mesh, in_specs=in_specs, out_specs=out_specs, check_vma=False)
```

```python
import math

import jax
import jax.numpy as jnp
import ml_dtypes
import numpy as np
from jax import lax
from jax.experimental import pallas as pl
from jax.experimental.pallas import tpu as pltpu
from jax.sharding import PartitionSpec as P

MESH = pl.DeviceIdType.MESH
F32 = jnp.float32
BF16 = jnp.bfloat16
N = 128
B = 8
G = 16
Q = 4
ZQ = B // Q
ROWS = B * ZQ
CHUNK = G * ROWS


def tables():
    k = np.arange(N)
    angle = 2.0 * math.pi * (np.outer(k, k) % N) / N
    c, s = np.cos(angle) / math.sqrt(N), np.sin(angle) / math.sqrt(N)
    fwd = np.block([[c, s], [-s, c]])
    inv = np.block([[c, -s], [s, c]])

    def pieces(m):
        hi = m.astype(np.float32).astype(ml_dtypes.bfloat16)
        lo = (m - hi.astype(np.float64)).astype(np.float32).astype(ml_dtypes.bfloat16)
        return [hi, hi, lo]

    one, chunk, slab = np.meshgrid(np.arange(ZQ), np.arange(Q), np.arange(G), indexing="ij")
    order = (slab * B + chunk * ZQ + one).reshape(-1)
    order = np.concatenate([order, order + N])
    return [
        np.concatenate(pieces(fwd), 1),
        np.concatenate(pieces(inv), 1),
        np.concatenate(pieces(inv), 0),
        np.concatenate(pieces(fwd), 0),
        np.concatenate(pieces(fwd[:, order]), 1),
        np.concatenate(pieces(inv[order]), 1),
    ]


def split(x):
    hi = x.astype(BF16)
    lo = (x - hi.astype(F32)).astype(BF16)
    return hi, lo


def left(table, x):
    hi, lo = split(x)
    return jnp.dot(table, jnp.concatenate([hi, lo, hi], 0), preferred_element_type=F32)


def right(x, table):
    hi, lo = split(x)
    return jnp.dot(jnp.concatenate([hi, lo, hi], 1), table, preferred_element_type=F32)


def loop(count, fn):
    def step(i, carry):
        fn(i)
        return carry

    lax.fori_loop(0, count, step, 0)


def shifted_sum(p0, p1, p2):
    lane = lax.broadcasted_iota(jnp.int32, p0.shape, 1)
    down = jnp.where(lane == 0, 0.0, pltpu.roll(p0, 1, 1))
    up = jnp.where(lane == N - 1, 0.0, pltpu.roll(p2, N - 1, 1))
    return p1 + down + up


def build_weights(wf, wm, wl, w1, w2, w3):
    lane = lax.broadcasted_iota(jnp.int32, (32, 512), 1)
    for dy in range(3):
        base = jnp.zeros((32, 512), F32)
        for dz in range(3):
            for dx in range(3):
                taps = wf[dz * 9 + dx * 3 + dy]
                for c in range(2):
                    base = jnp.where(lane == dz * 48 + c * 24 + dx + 5, taps[:, c:c + 1], base)
        hi = base.astype(BF16).astype(F32)
        full = hi + pltpu.roll(hi, 144, 1) + pltpu.roll(base - hi, 288, 1)
        for xo in range(12):
            r = (dy * 12 + xo) * 32
            w1[r:r + 32, :] = (pltpu.roll(full, xo, 1) if xo else full).astype(BF16)
    for dz in range(3):
        for dy in range(3):
            base = jnp.concatenate(
                [wm[dz * 9 + dx * 3 + dy] for dx in range(3)] + [jnp.zeros((32, 160), F32)], 1)
            for xo in range(5):
                hi, lo = split(pltpu.roll(base, 32 * xo, 1) if xo else base)
                r = (dy * 5 + xo) * 32
                w2[r:r + 32, dz * 768:dz * 768 + 256] = hi
                w2[r:r + 32, dz * 768 + 256:dz * 768 + 512] = hi
                w2[r:r + 32, dz * 768 + 512:dz * 768 + 768] = lo
    for dz in range(3):
        for dy in range(3):
            base = jnp.concatenate(
                [wl[dz * 9 + dx * 3 + dy] for dx in range(3)] + [jnp.zeros((2, 416), F32)], 1)
            both = jnp.concatenate([jnp.broadcast_to(base[o:o + 1], (8, 512)) for o in range(2)], 0)
            row = lax.broadcasted_iota(jnp.int32, (16, 512), 0) % 8
            moved = both
            for xo in range(1, 8):
                moved = jnp.where(row == xo, pltpu.roll(both, 32 * xo, 1), moved)
            hi, lo = split(moved[:, :384])
            r = dz * 48 + dy * 16
            w3[r:r + 16, :] = hi
            w3[144 + r:160 + r, :] = lo


def kernel(
    est_in, maps_in, meas_in, mask_in, wf_in, wm_in, wl_in, t0, t1, t2, t3, t4, t5,
    combined, refined,
    est, maps, meas, mask, wf, wm, wl, lf, li, rf, ri_, lzf, lzi,
    gath, send1, recv1, send2, recv2, part, rs_a, rs_b,
    w1, w2, w3, big, f0h, f0l, f1h, f1l, f2h, f2l, q3,
    load_sem, ag_send, ag_recv, a1_send, a1_recv, a2_send, a2_recv,
    sib_send, sib_recv, rs_send, rs_recv, halo_send, halo_recv,
):
    me_c = lax.axis_index("coil")
    me_s = lax.axis_index("slab")
    core = lax.rem(me_c, 2)
    chip = me_c // 2
    sibling = me_c + 1 - 2 * core

    barrier = pltpu.get_barrier_semaphore()

    def near_id(dz, dx):
        return {"coil": lax.rem(me_c + dx + G, G), "slab": lax.rem(me_s + dz + G, G)}

    def greet(k):
        pl.semaphore_signal(barrier, inc=1, device_id={"coil": lax.rem(me_c + k + 1, G)}, device_id_type=MESH)
        pl.semaphore_signal(barrier, inc=1, device_id={"slab": lax.rem(me_s + k + 1, G)}, device_id_type=MESH)

    loop(G - 1, greet)
    for dz in (-1, 1):
        for dx in (-1, 1):
            pl.semaphore_signal(barrier, inc=1, device_id=near_id(dz, dx), device_id_type=MESH)

    pairs = [(est_in, est), (t0, lf), (maps_in, maps), (wf_in, wf), (wm_in, wm), (wl_in, wl), (t2, rf), (t4, lzf),
             (meas_in, meas), (mask_in, mask), (t5, lzi), (t3, ri_), (t1, li)]
    loads = [pltpu.make_async_copy(a, b, load_sem.at[i]) for i, (a, b) in enumerate(pairs)]
    for load in loads:
        load.start()
    pl.semaphore_wait(barrier, 2 * (G - 1) + 4)

    def ag_copy(src, q, slot, target):
        return pltpu.make_async_remote_copy(
            src_ref=src, dst_ref=gath.at[q, slot], send_sem=ag_send, recv_sem=ag_recv.at[q, slot],
            device_id={"coil": target}, device_id_type=MESH)

    loads[0].wait()
    for q in range(Q):
        mine = est.at[:, pl.ds(q * ZQ, ZQ)]

        def ag_out(k):
            ag_copy(mine, q, me_c, 2 * lax.rem(chip + k + 1, 8) + core).start()

        loop(7, ag_out)
        ag_copy(mine, q, me_c, sibling).start()
        gath[q, me_c] = est[:, q * ZQ:(q + 1) * ZQ]

    def forward(q):
        def ag_in(k):
            slot = 2 * lax.rem(chip + 7 - k, 8) + core
            ag_copy(gath.at[q, slot], q, slot, sibling).wait_recv()
            ag_copy(gath.at[q, slot], q, slot, sibling).start()

        loop(7, ag_in)

    def exchange(buf, dst, c, q, peer, slot, send_sem, recv_sem):
        return pltpu.make_async_remote_copy(
            src_ref=buf.at[c, :, pl.ds(pl.multiple_of(q * CHUNK + peer * ROWS, ROWS), ROWS), :],
            dst_ref=dst.at[c, :, pl.ds(pl.multiple_of(q * CHUNK + slot * ROWS, ROWS), ROWS), :],
            send_sem=send_sem, recv_sem=recv_sem.at[c, q],
            device_id={"slab": peer}, device_id_type=MESH)

    def exchange_out(buf, dst, c, q, send_sem, recv_sem):
        def out(k):
            exchange(buf, dst, c, q, lax.rem(me_s + k + 1, G), me_s, send_sem, recv_sem).start()

        loop(G - 1, out)
        own = pl.ds(pl.multiple_of(q * CHUNK + me_s * ROWS, ROWS), ROWS)
        for r in range(2):
            dst[c, r, own, :] = buf[c, r, own, :]

    def all_of(buf, c, q):
        return buf.at[c, :, pl.ds(pl.multiple_of(q * CHUNK, CHUNK), CHUNK - ROWS), :]

    def exchange_in(dst, c, q, recv_sem):
        ref = all_of(dst, c, q)
        pltpu.make_async_copy(ref, ref, recv_sem.at[c, q]).wait()

    def slab_chunk(c, q):
        cols = []
        for j in range(ZQ):
            z = q * ZQ + j
            ir = gath[q, :, 0, j].reshape(N, N)
            ii = gath[q, :, 1, j].reshape(N, N)
            mr = maps[c, 0, z]
            mi = maps[c, 1, z]
            cols.append(jnp.concatenate([mr * ir - mi * ii, mr * ii + mi * ir], 0))
        y = left(lf[...], jnp.concatenate(cols, 1))
        for j in range(ZQ):
            for r in range(2):
                send1[c, r, pl.ds(q * CHUNK + j, N, stride=ZQ), :] = y[r * N:(r + 1) * N, j * N:(j + 1) * N]
        exchange_out(send1, recv1, c, q, a1_send, a1_recv)

    forward(0)
    for q in range(Q):
        def ag_last(k):
            slot = 2 * lax.rem(chip + 8 - k, 8) + 1 - core
            ag_copy(gath.at[q, slot], q, slot, sibling).wait_recv()

        loop(8, ag_last)
        if q == 0:
            loads[1].wait()
            loads[2].wait()
        slab_chunk(0, q)
        if q + 1 < Q:
            forward(q + 1)
    loop(Q, lambda q: slab_chunk(1, q))

    for load in loads[3:]:
        load.wait()
    build_weights(wf, wm, wl, w1, w2, w3)
    f1h[384:, :] = jnp.zeros((32, 12 * N), BF16)
    f1l[384:, :] = jnp.zeros((32, 12 * N), BF16)

    def pencils(c):
        loop(Q, lambda q: exchange_in(recv1, c, q, a1_recv))

        def pair(kp):
            rows = []
            for j in range(2):
                halves = []
                for r in range(2):
                    halves.append(jnp.concatenate([
                        recv1[c, r, pl.ds((2 * kp + j) * ZQ + i, Q * G, stride=ROWS), :] for i in range(ZQ)], 0))
                rows.append(jnp.concatenate(halves, 1))
            y = right(jnp.concatenate(rows, 0), rf[...])
            x = jnp.concatenate([
                jnp.concatenate([y[:N, :N], y[N:, :N]], 1),
                jnp.concatenate([y[:N, N:], y[N:, N:]], 1)], 0)
            x = left(lzf[...], x)
            w = jnp.where(mask[...] == 1, 0.5, 0.0)
            halves = []
            for r in range(2):
                pieces = []
                for j in range(2):
                    k = x[r * N:(r + 1) * N, j * N:(j + 1) * N]
                    m = meas[c, r, pl.ds(2 * kp + j, N, stride=B), :]
                    pieces.append(k - w * (k - m))
                halves.append(jnp.concatenate(pieces, 1))
            x = left(lzi[...], jnp.concatenate(halves, 0))
            y = jnp.concatenate([
                jnp.concatenate([x[:N, :N], x[N:, :N]], 1),
                jnp.concatenate([x[:N, N:], x[N:, N:]], 1)], 0)
            y = right(y, ri_[...])
            for j in range(2):
                for r in range(2):
                    for i in range(ZQ):
                        send2[c, r, pl.ds((2 * kp + j) * ZQ + i, Q * G, stride=ROWS), :] = (
                            y[j * N + i * Q * G:j * N + (i + 1) * Q * G, r * N:(r + 1) * N])

        loop(4, pair)
        loop(Q, lambda p: exchange_out(send2, recv2, c, p, a2_send, a2_recv))

    loop(2, pencils)

    def to_sibling(p):
        return pltpu.make_async_remote_copy(
            src_ref=part.at[p, 1 - core], dst_ref=rs_a.at[p], send_sem=sib_send, recv_sem=sib_recv.at[p],
            device_id={"coil": sibling}, device_id_type=MESH)

    def rs_copy(p, target, slot):
        return pltpu.make_async_remote_copy(
            src_ref=rs_a.at[p, target], dst_ref=rs_b.at[p, slot], send_sem=rs_send, recv_sem=rs_recv.at[p],
            device_id={"coil": 2 * target + core}, device_id_type=MESH)

    def finish(p):
        exchange_in(recv2, 0, p, a2_recv)
        exchange_in(recv2, 1, p, a2_recv)
        sums = [[None, None] for j in range(ZQ)]
        for c in range(2):
            cols = []
            for j in range(ZQ):
                at = pl.ds(p * CHUNK + j, N, stride=ZQ)
                cols.append(jnp.concatenate([recv2[c, 0, at, :], recv2[c, 1, at, :]], 0))
            x = left(li[...], jnp.concatenate(cols, 1))
            for j in range(ZQ):
                z = p * ZQ + j
                br = x[:N, j * N:(j + 1) * N]
                bi = x[N:, j * N:(j + 1) * N]
                mr = maps[c, 0, z]
                mi = maps[c, 1, z]
                now = (mr * br + mi * bi, mr * bi - mi * br)
                for r in range(2):
                    sums[j][r] = now[r] if c == 0 else sums[j][r] + now[r]
        for j in range(ZQ):
            for r in range(2):
                v = sums[j][r].reshape(8, 2, B, N)
                for g in range(2):
                    part[p, g, :, r, j] = v[:, g]
        to_sibling(p).start()
        to_sibling(p).wait_recv()

        def rs_out(k):
            target = lax.rem(chip + k + 1, 8)
            rs_a[p, target] = rs_a[p, target] + part[p, core, target]
            rs_copy(p, target, chip).start()

        loop(7, rs_out)
        rs_b[p, chip] = rs_a[p, chip] + part[p, core, chip]
        ref = rs_b.at[p, pl.ds(0, 7)]
        pltpu.make_async_copy(ref, ref, rs_recv.at[p]).wait()
        total = rs_b[p, 0]
        for k in range(1, 8):
            total = total + rs_b[p, k]
        combined[:, pl.ds(p * ZQ, ZQ)] = total
        big[1, :, pl.ds(3 + p * ZQ, ZQ)] = total

    loop(Q, finish)

    near = [(a, b) for a in (-1, 0, 1) for b in (-1, 0, 1) if (a, b) != (0, 0)]
    source = {-1: (3, 3), 0: (3, 8), 1: (8, 3)}
    place = {-1: (11, 3), 0: (3, 8), 1: (0, 3)}
    copies = []
    for i, (dz, dx) in enumerate(near):
        a, n = source[dz]
        b, n = place[dz]
        copies.append(pltpu.make_async_remote_copy(
            src_ref=big.at[1, :, pl.ds(a, n)], dst_ref=big.at[1 - dx, :, pl.ds(b, n)],
            send_sem=halo_send.at[i], recv_sem=halo_recv.at[i],
            device_id=near_id(dz, dx), device_id_type=MESH))
        copies[-1].start()
    for copy in copies:
        copy.wait_recv()

    for z in range(14):
        rows = []
        for c in range(2):
            for blk in range(3):
                v = big[blk, c, z]
                if blk == 0:
                    v = jnp.where(me_c == 0, 0.0, v)
                if blk == 2:
                    v = jnp.where(me_c == G - 1, 0.0, v)
                if z < 3:
                    v = jnp.where(me_s == 0, 0.0, v)
                if z >= 11:
                    v = jnp.where(me_s == G - 1, 0.0, v)
                rows.append(v)
        hi, lo = split(jnp.concatenate(rows, 0))
        f0h[:, z * N:(z + 1) * N] = hi
        f0l[:, z * N:(z + 1) * N] = lo

    def inside(rows, first_x, z):
        x = me_c * B + first_x + lax.broadcasted_iota(jnp.int32, (rows, N), 0) // 32
        z = me_s * B + z
        return (x >= 0) & (x < N) & (z >= 0) & (z < N)

    def conv1(i):
        def planes(ref):
            return [ref[:, pl.ds(pl.multiple_of((2 * i + dz) * N, N), 2 * N)] for dz in range(3)]

        hi = planes(f0h)
        y = jnp.dot(w1[:, 0:432], jnp.concatenate(hi + planes(f0l) + hi, 0), preferred_element_type=F32)
        for j in range(2):
            p = [y[d * 384:(d + 1) * 384, j * N:(j + 1) * N] for d in range(3)]
            v = jnp.maximum(shifted_sum(*p), 0.0)
            v = jnp.where(inside(384, -2, 2 * i + j - 2), v, 0.0)
            hi_out, lo_out = split(v)
            at = pl.ds(pl.multiple_of((2 * i + j) * N, N), N)
            f1h[0:384, at] = hi_out
            f1l[0:384, at] = lo_out

    loop(6, conv1)

    def conv2(i):
        for g in range(2):
            parts = []
            for dz in range(3):
                at = pl.ds(pl.multiple_of((2 * i + dz) * N, N), 2 * N)
                hi = f1h[g * 160:g * 160 + 256, at]
                parts += [hi, f1l[g * 160:g * 160 + 256, at], hi]
            y = jnp.dot(w2[...], jnp.concatenate(parts, 0), preferred_element_type=F32)
            for j in range(2):
                p = [y[d * 160:(d + 1) * 160, j * N:(j + 1) * N] for d in range(3)]
                v = jnp.maximum(shifted_sum(*p), 0.0)
                v = jnp.where(inside(160, g * 5 - 1, 2 * i + j - 1), v, 0.0)
                hi, lo = split(v)
                at = pl.ds(pl.multiple_of((2 * i + j) * N, N), N)
                f2h[g * 160:(g + 1) * 160, at] = hi
                f2l[g * 160:(g + 1) * 160, at] = lo

    loop(5, conv2)

    def conv3(i):
        at = pl.ds(pl.multiple_of(2 * i * N, N), 2 * N)
        y = jnp.dot(w3[:, 0:320], f2h[:, at], preferred_element_type=F32)
        y = y[:144] + y[144:] + jnp.dot(w3[0:144, 0:320], f2l[:, at], preferred_element_type=F32)
        q3[2 * i] = y[:, :N]
        q3[2 * i + 1] = y[:, N:]

    loop(5, conv3)

    def last(z):
        p = []
        for dy in range(3):
            p.append(sum(q3[z + dz, dz * 48 + dy * 16:dz * 48 + dy * 16 + 16, :] for dz in range(3)))
        v = shifted_sum(*p)
        refined[0, z] = combined[0, z] + v[:B]
        refined[1, z] = combined[1, z] + v[B:]

    loop(B, last)

    for copy in copies:
        copy.wait_send()

    def drain(ref, sem):
        pltpu.make_async_copy(ref, ref, sem).wait()

    drain(gath.at[:, pl.ds(0, G - 1)], ag_send)
    drain(send1.at[:, :, pl.ds(0, Q * (CHUNK - ROWS))], a1_send)
    drain(send2.at[:, :, pl.ds(0, Q * (CHUNK - ROWS))], a2_send)
    drain(part.at[:, 0], sib_send)
    drain(rs_a.at[:, pl.ds(0, 7)], rs_send)


def body(estimate, coil_maps, measured, line_mask, w_first, w_middle, w_last):
    tabs = [jnp.asarray(t) for t in tables()]
    measured = measured.reshape(2, 2, N * B, N)
    operands = (estimate, coil_maps, measured, line_mask, w_first, w_middle, w_last, *tabs)
    vmem = pl.BlockSpec(memory_space=pltpu.VMEM)
    dma = pltpu.SemaphoreType.DMA
    block = jax.ShapeDtypeStruct((2, B, B, N), F32)
    return pl.pallas_call(
        kernel,
        out_shape=(block, block),
        in_specs=[pl.BlockSpec(memory_space=pl.ANY)] * len(operands),
        out_specs=(vmem, vmem),
        scratch_shapes=[pltpu.VMEM(a.shape, a.dtype) for a in (
            estimate, coil_maps, measured, line_mask, w_first, w_middle, w_last,
            tabs[0], tabs[1], tabs[2], tabs[3], tabs[4], tabs[5])] + [
            pltpu.VMEM((Q, G, 2, ZQ, B, N), F32),
            pltpu.VMEM((2, 2, N * B, N), F32),
            pltpu.VMEM((2, 2, N * B, N), F32),
            pltpu.VMEM((2, 2, N * B, N), F32),
            pltpu.VMEM((2, 2, N * B, N), F32),
            pltpu.VMEM((Q, 2, 8, 2, ZQ, B, N), F32),
            pltpu.VMEM((Q, 8, 2, ZQ, B, N), F32),
            pltpu.VMEM((Q, 8, 2, ZQ, B, N), F32),
            pltpu.VMEM((1152, 512), BF16),
            pltpu.VMEM((480, 2304), BF16),
            pltpu.VMEM((288, 384), BF16),
            pltpu.VMEM((3, 2, 14, B, N), F32),
            pltpu.VMEM((48, 14 * N), BF16), pltpu.VMEM((48, 14 * N), BF16),
            pltpu.VMEM((416, 12 * N), BF16), pltpu.VMEM((416, 12 * N), BF16),
            pltpu.VMEM((320, 10 * N), BF16), pltpu.VMEM((320, 10 * N), BF16),
            pltpu.VMEM((10, 144, N), F32),
            dma((13,)), dma, dma((Q, G)), dma, dma((2, Q)), dma, dma((2, Q)),
            dma, dma((Q,)), dma, dma((Q,)), dma((8,)), dma((8,)),
        ],
        compiler_params=pltpu.CompilerParams(
            collective_id=0, has_side_effects=True, vmem_limit_bytes=56 * 2**20),
    )(*operands)


def solution(mesh):
    in_specs = (
        P(None, "slab", "coil", None),
        P("coil", None, "slab", None, None),
        P("coil", None, None, "slab", None),
        P(),
        P(),
        P(),
        P(),
    )
    out_specs = (P(None, "slab", "coil", None), P(None, "slab", "coil", None))
    return jax.shard_map(body, mesh=mesh, in_specs=in_specs, out_specs=out_specs, check_vma=False)
```

```python
import math

import jax
import jax.numpy as jnp
import ml_dtypes
import numpy as np
from jax import lax
from jax.experimental import pallas as pl
from jax.experimental.pallas import tpu as pltpu
from jax.sharding import PartitionSpec as P

MESH = pl.DeviceIdType.MESH
F32 = jnp.float32
BF16 = jnp.bfloat16
N = 128
B = 8
G = 16
Q = 4
ZQ = B // Q
ROWS = B * ZQ
CHUNK = G * ROWS


def tables():
    k = np.arange(N)
    angle = 2.0 * math.pi * (np.outer(k, k) % N) / N
    c, s = np.cos(angle) / math.sqrt(N), np.sin(angle) / math.sqrt(N)
    fwd = np.block([[c, s], [-s, c]])
    inv = np.block([[c, -s], [s, c]])

    def pieces(m):
        hi = m.astype(np.float32).astype(ml_dtypes.bfloat16)
        lo = (m - hi.astype(np.float64)).astype(np.float32).astype(ml_dtypes.bfloat16)
        return [hi, hi, lo]

    one, chunk, slab = np.meshgrid(np.arange(ZQ), np.arange(Q), np.arange(G), indexing="ij")
    order = (slab * B + chunk * ZQ + one).reshape(-1)
    order = np.concatenate([order, order + N])
    return [
        np.concatenate(pieces(fwd), 1),
        np.concatenate(pieces(inv), 1),
        np.concatenate(pieces(inv), 0),
        np.concatenate(pieces(fwd), 0),
        np.concatenate(pieces(fwd[:, order]), 1),
        np.concatenate(pieces(inv[order]), 1),
    ]


def split(x):
    hi = x.astype(BF16)
    lo = (x - hi.astype(F32)).astype(BF16)
    return hi, lo


def left(table, x):
    hi, lo = split(x)
    return jnp.dot(table, jnp.concatenate([hi, lo, hi], 0), preferred_element_type=F32)


def right(x, table):
    hi, lo = split(x)
    return jnp.dot(jnp.concatenate([hi, lo, hi], 1), table, preferred_element_type=F32)


def loop(count, fn):
    def step(i, carry):
        fn(i)
        return carry

    lax.fori_loop(0, count, step, 0)


def shifted_sum(p0, p1, p2):
    lane = lax.broadcasted_iota(jnp.int32, p0.shape, 1)
    down = jnp.where(lane == 0, 0.0, pltpu.roll(p0, 1, 1))
    up = jnp.where(lane == N - 1, 0.0, pltpu.roll(p2, N - 1, 1))
    return p1 + down + up


def build_weights(wf, wm, wl, w1, w2, w3):
    lane = lax.broadcasted_iota(jnp.int32, (32, 512), 1)
    for dy in range(3):
        base = jnp.zeros((32, 512), F32)
        for dz in range(3):
            for dx in range(3):
                taps = jnp.transpose(jnp.concatenate([wf[dz * 9 + dx * 3 + dy], jnp.zeros((6, 32), F32)], 0))
                for c in range(2):
                    base = jnp.where(lane == dz * 48 + c * 24 + dx + 5, taps[:, c:c + 1], base)
        hi = base.astype(BF16).astype(F32)
        full = hi + pltpu.roll(hi, 144, 1) + pltpu.roll(base - hi, 288, 1)
        for xo in range(12):
            r = xo // 4 * 384 + dy * 128 + xo % 4 * 32
            w1[r:r + 32, :] = (pltpu.roll(full, xo, 1) if xo else full).astype(BF16)
    for dz in range(3):
        for dy in range(3):
            base = jnp.concatenate(
                [wm[dz * 9 + dx * 3 + dy] for dx in range(3)] + [jnp.zeros((32, 32), F32)], 1)
            for xo in range(2):
                hi, lo = split(pltpu.roll(base, 32, 1) if xo else base)
                r = (dy * 2 + xo) * 32
                for part, value in enumerate((hi, hi, lo)):
                    w2[r:r + 32, part * 384 + dz * 128:part * 384 + dz * 128 + 128] = value
    for dz in range(3):
        for dy in range(3):
            base = jnp.concatenate(
                [wl[dz * 9 + dx * 3 + dy] for dx in range(3)] + [jnp.zeros((2, 416), F32)], 1)
            both = jnp.concatenate([jnp.broadcast_to(base[o:o + 1], (8, 512)) for o in range(2)], 0)
            row = lax.broadcasted_iota(jnp.int32, (16, 512), 0) % 8
            moved = both
            for xo in range(1, 8):
                moved = jnp.where(row == xo, pltpu.roll(both, 32 * xo, 1), moved)
            hi, lo = split(moved[:, :384])
            r = dz * 48 + dy * 16
            w3[r:r + 16, :] = hi
            w3[144 + r:160 + r, :] = lo


def kernel(
    est_in, maps_in, meas_in, mask_in, wf_in, wm_in, wl_in, t0, t1, t2, t3, t4, t5,
    combined, refined,
    est, maps, meas, mask, wf, wm, wl, lf, li, rf, ri_, lzf, lzi,
    gath, send1, recv1, send2, recv2, part, rs_a, rs_b,
    w1, w2, w3, big, f0h, f0l, f1h, f1l, f2h, f2l, q3,
    load_sem, ag_send, ag_recv, a1_send, a1_recv, a2_send, a2_recv,
    sib_send, sib_recv, rs_send, rs_recv, halo_send, halo_recv,
):
    me_c = lax.axis_index("coil")
    me_s = lax.axis_index("slab")
    core = lax.rem(me_c, 2)
    chip = me_c // 2
    sibling = me_c + 1 - 2 * core

    barrier = pltpu.get_barrier_semaphore()

    def near_id(dz, dx):
        return {"coil": lax.rem(me_c + dx + G, G), "slab": lax.rem(me_s + dz + G, G)}

    def greet(k):
        pl.semaphore_signal(barrier, inc=1, device_id={"coil": lax.rem(me_c + k + 1, G)}, device_id_type=MESH)
        pl.semaphore_signal(barrier, inc=1, device_id={"slab": lax.rem(me_s + k + 1, G)}, device_id_type=MESH)

    loop(G - 1, greet)
    for dz in (-1, 1):
        for dx in (-1, 1):
            pl.semaphore_signal(barrier, inc=1, device_id=near_id(dz, dx), device_id_type=MESH)

    pairs = [(est_in, est), (t0, lf), (maps_in, maps), (wf_in, wf), (wm_in, wm), (wl_in, wl), (t2, rf), (t4, lzf),
             (meas_in, meas), (mask_in, mask), (t5, lzi), (t3, ri_), (t1, li)]
    loads = [pltpu.make_async_copy(a, b, load_sem.at[i]) for i, (a, b) in enumerate(pairs)]
    for load in loads:
        load.start()
    pl.semaphore_wait(barrier, 2 * (G - 1) + 4)

    def ag_copy(src, q, slot, target):
        return pltpu.make_async_remote_copy(
            src_ref=src, dst_ref=gath.at[q, slot], send_sem=ag_send, recv_sem=ag_recv.at[q, slot],
            device_id={"coil": target}, device_id_type=MESH)

    def gather_out(q):
        mine = est.at[:, pl.ds(q * ZQ, ZQ)]

        def ag_out(k):
            ag_copy(mine, q, me_c, 2 * lax.rem(chip + k + 1, 8) + core).start()

        loop(7, ag_out)
        ag_copy(mine, q, me_c, sibling).start()
        gath[q, me_c] = est[:, q * ZQ:(q + 1) * ZQ]

    def forward(q):
        def ag_in(k):
            slot = 2 * lax.rem(chip + 7 - k, 8) + core
            ag_copy(gath.at[q, slot], q, slot, sibling).wait_recv()
            ag_copy(gath.at[q, slot], q, slot, sibling).start()

        loop(7, ag_in)

    def exchange(buf, dst, c, q, peer, slot, send_sem, recv_sem):
        return pltpu.make_async_remote_copy(
            src_ref=buf.at[c, :, pl.ds(pl.multiple_of(q * CHUNK + peer * ROWS, ROWS), ROWS), :],
            dst_ref=dst.at[c, :, pl.ds(pl.multiple_of(q * CHUNK + slot * ROWS, ROWS), ROWS), :],
            send_sem=send_sem, recv_sem=recv_sem.at[c, q],
            device_id={"slab": peer}, device_id_type=MESH)

    def exchange_out(buf, dst, c, q, send_sem, recv_sem):
        def out(k):
            exchange(buf, dst, c, q, lax.rem(me_s + k + 1, G), me_s, send_sem, recv_sem).start()

        loop(G - 1, out)
        own = pl.ds(pl.multiple_of(q * CHUNK + me_s * ROWS, ROWS), ROWS)
        for r in range(2):
            dst[c, r, own, :] = buf[c, r, own, :]

    def all_of(buf, c, q):
        return buf.at[c, :, pl.ds(pl.multiple_of(q * CHUNK, CHUNK), CHUNK - ROWS), :]

    def exchange_in(dst, c, q, recv_sem):
        ref = all_of(dst, c, q)
        pltpu.make_async_copy(ref, ref, recv_sem.at[c, q]).wait()

    def slab_chunk(c, q):
        cols = []
        for j in range(ZQ):
            z = q * ZQ + j
            ir = gath[q, :, 0, j].reshape(N, N)
            ii = gath[q, :, 1, j].reshape(N, N)
            mr = maps[c, 0, z]
            mi = maps[c, 1, z]
            cols.append(jnp.concatenate([mr * ir - mi * ii, mr * ii + mi * ir], 0))
        y = left(lf[...], jnp.concatenate(cols, 1))
        for j in range(ZQ):
            for r in range(2):
                send1[c, r, pl.ds(q * CHUNK + j, N, stride=ZQ), :] = y[r * N:(r + 1) * N, j * N:(j + 1) * N]
        exchange_out(send1, recv1, c, q, a1_send, a1_recv)

    loads[0].wait()
    gather_out(0)
    for q in range(Q):
        forward(q)
        if q + 1 < Q:
            gather_out(q + 1)

        def ag_last(k):
            slot = 2 * lax.rem(chip + 8 - k, 8) + 1 - core
            ag_copy(gath.at[q, slot], q, slot, sibling).wait_recv()

        loop(8, ag_last)
        if q == 0:
            loads[1].wait()
            loads[2].wait()
        slab_chunk(0, q)
    loop(Q, lambda q: slab_chunk(1, q))

    for load in loads[3:]:
        load.wait()
    build_weights(wf, wm, wl, w1, w2, w3)

    def pencils(c):
        loop(Q, lambda q: exchange_in(recv1, c, q, a1_recv))

        def pair(kp):
            rows = []
            for j in range(2):
                halves = []
                for r in range(2):
                    halves.append(jnp.concatenate([
                        recv1[c, r, pl.ds((2 * kp + j) * ZQ + i, Q * G, stride=ROWS), :] for i in range(ZQ)], 0))
                rows.append(jnp.concatenate(halves, 1))
            y = right(jnp.concatenate(rows, 0), rf[...])
            x = jnp.concatenate([
                jnp.concatenate([y[:N, :N], y[N:, :N]], 1),
                jnp.concatenate([y[:N, N:], y[N:, N:]], 1)], 0)
            x = left(lzf[...], x)
            w = jnp.where(mask[...] == 1, 0.5, 0.0)
            halves = []
            for r in range(2):
                pieces = []
                for j in range(2):
                    k = x[r * N:(r + 1) * N, j * N:(j + 1) * N]
                    m = meas[c, r, pl.ds(2 * kp + j, N, stride=B), :]
                    pieces.append(k - w * (k - m))
                halves.append(jnp.concatenate(pieces, 1))
            x = left(lzi[...], jnp.concatenate(halves, 0))
            y = jnp.concatenate([
                jnp.concatenate([x[:N, :N], x[N:, :N]], 1),
                jnp.concatenate([x[:N, N:], x[N:, N:]], 1)], 0)
            y = right(y, ri_[...])
            for j in range(2):
                for r in range(2):
                    for i in range(ZQ):
                        send2[c, r, pl.ds((2 * kp + j) * ZQ + i, Q * G, stride=ROWS), :] = (
                            y[j * N + i * Q * G:j * N + (i + 1) * Q * G, r * N:(r + 1) * N])

        loop(4, pair)
        loop(Q, lambda p: exchange_out(send2, recv2, c, p, a2_send, a2_recv))

    loop(2, pencils)

    def to_sibling(p):
        return pltpu.make_async_remote_copy(
            src_ref=part.at[p, 1 - core], dst_ref=rs_a.at[p], send_sem=sib_send, recv_sem=sib_recv.at[p],
            device_id={"coil": sibling}, device_id_type=MESH)

    def rs_copy(p, target, slot):
        return pltpu.make_async_remote_copy(
            src_ref=rs_a.at[p, target], dst_ref=rs_b.at[p, slot], send_sem=rs_send, recv_sem=rs_recv.at[p],
            device_id={"coil": 2 * target + core}, device_id_type=MESH)

    def coil_back(c, p):
        exchange_in(recv2, c, p, a2_recv)
        cols = []
        for j in range(ZQ):
            at = pl.ds(p * CHUNK + j, N, stride=ZQ)
            cols.append(jnp.concatenate([recv2[c, 0, at, :], recv2[c, 1, at, :]], 0))
        x = left(li[...], jnp.concatenate(cols, 1))
        for j in range(ZQ):
            z = p * ZQ + j
            br = x[:N, j * N:(j + 1) * N]
            bi = x[N:, j * N:(j + 1) * N]
            mr = maps[c, 0, z]
            mi = maps[c, 1, z]
            for r, v in enumerate((mr * br + mi * bi, mr * bi - mi * br)):
                v = v.reshape(8, 2, B, N)
                for g in range(2):
                    part[p, g, :, r, j] = v[:, g] if c == 0 else part[p, g, :, r, j] + v[:, g]

    near = [(a, b) for a in (-1, 0, 1) for b in (-1, 0, 1) if (a, b) != (0, 0)]

    def halo(dz, dx, p=0):
        a, b, n = {-1: (3, 11, 3), 0: (3 + p * ZQ, 3 + p * ZQ, ZQ), 1: (8, 0, 3)}[dz]
        i = 3 * (dz > 0) + 6 * (dz == 0) + (dx + 1 if dz else p * 2 + (dx + 1) // 2)
        return pltpu.make_async_remote_copy(
            src_ref=big.at[1, :, pl.ds(a, n)], dst_ref=big.at[1 - dx, :, pl.ds(b, n)],
            send_sem=halo_send.at[i], recv_sem=halo_recv.at[i],
            device_id=near_id(dz, dx), device_id_type=MESH)

    def spread(p):
        def rs_out(k):
            target = lax.rem(chip + k + 1, 8)
            rs_a[p, target] = rs_a[p, target] + part[p, core, target]
            rs_copy(p, target, chip).start()

        to_sibling(p).wait_recv()
        loop(7, rs_out)
        rs_b[p, chip] = rs_a[p, chip] + part[p, core, chip]

    def total(p):
        ref = rs_b.at[p, pl.ds(0, 7)]
        pltpu.make_async_copy(ref, ref, rs_recv.at[p]).wait()
        value = rs_b[p, 0]
        for k in range(1, 8):
            value = value + rs_b[p, k]
        big[1, :, 3 + p * ZQ:3 + (p + 1) * ZQ] = value
        halo(0, -1, p).start()
        halo(0, 1, p).start()
        if p in (1, 3):
            for dx in (0, -1, 1):
                halo(p - 2, dx).start()
        combined[:, p * ZQ:(p + 1) * ZQ] = value

    loop(Q, lambda p: coil_back(0, p))
    for p in range(Q):
        coil_back(1, p)
        to_sibling(p).start()
        if p:
            total(p - 1)
        spread(p)
    total(Q - 1)

    low_c, high_c, low_s, high_s = me_c == 0, me_c == G - 1, me_s == 0, me_s == G - 1

    def guard(v, *outside):
        for out, here in outside:
            if here:
                v = jnp.where(out, 0.0, v)
        return v

    def layer0(z):
        rows = []
        for c in range(2):
            for blk in range(3):
                rows.append(guard(
                    big[blk, c, z], (low_c, blk == 0), (high_c, blk == 2), (low_s, z < 3), (high_s, z >= 11)))
        f0h[:, z * N:(z + 1) * N], f0l[:, z * N:(z + 1) * N] = split(jnp.concatenate(rows, 0))

    def window(hi, lo, i, rows):
        h = [hi[rows, (2 * i + dz) * N:(2 * i + dz + 2) * N] for dz in range(3)]
        l = [lo[rows, (2 * i + dz) * N:(2 * i + dz + 2) * N] for dz in range(3)]
        return jnp.concatenate(h + l + h, 0)

    def conv1(i):
        data = window(f0h, f0l, i, slice(0, 48))
        for g in range(3):
            y = jnp.dot(w1[g * 384:(g + 1) * 384, 0:432], data, preferred_element_type=F32)
            for j in range(2):
                z = 2 * i + j
                v = jnp.maximum(shifted_sum(*[y[d * 128:(d + 1) * 128, j * N:(j + 1) * N] for d in range(3)]), 0.0)
                v = guard(v, (low_s, z < 2), (high_s, z >= 10))
                v = jnp.concatenate([
                    guard(v[:64], (low_c, g == 0)), guard(v[64:], (high_c, g == 2))], 0)
                at = (slice(g * 128, (g + 1) * 128), slice(z * N, (z + 1) * N))
                f1h[at], f1l[at] = split(v)

    def conv2(i):
        for g in range(5):
            data = window(f1h, f1l, i, slice(g * 64, g * 64 + 128))
            y = jnp.dot(w2[...], data, preferred_element_type=F32)
            for j in range(2):
                z = 2 * i + j
                v = jnp.maximum(shifted_sum(*[y[d * 64:(d + 1) * 64, j * N:(j + 1) * N] for d in range(3)]), 0.0)
                v = guard(v, (low_s, z < 1), (high_s, z >= 9))
                v = jnp.concatenate([
                    guard(v[:32], (low_c, g == 0)), guard(v[32:], (high_c, g == 4))], 0)
                at = (slice(g * 64, (g + 1) * 64), slice(z * N, (z + 1) * N))
                f2h[at], f2l[at] = split(v)

    def conv3(i):
        at = slice(2 * i * N, (2 * i + 2) * N)
        y = jnp.dot(w3[:, 0:320], f2h[:, at], preferred_element_type=F32)
        y = y[:144] + y[144:] + jnp.dot(w3[0:144, 0:320], f2l[:, at], preferred_element_type=F32)
        q3[2 * i] = y[:, :N]
        q3[2 * i + 1] = y[:, N:]

    for p in range(3):
        halo(0, -1, p).wait_recv()
        halo(0, 1, p).wait_recv()
    for z in range(3, 9):
        layer0(z)
    conv1(2)
    for dx in (-1, 0, 1):
        halo(-1, dx).wait_recv()
    for z in range(11, 14):
        layer0(z)
    halo(0, -1, 3).wait_recv()
    halo(0, 1, 3).wait_recv()
    layer0(9)
    layer0(10)
    for i in (3, 4, 5):
        conv1(i)
    for i in (2, 3, 4):
        conv2(i)
    for i in (2, 3, 4):
        conv3(i)
    for dx in (-1, 0, 1):
        halo(1, dx).wait_recv()
    for z in range(3):
        layer0(z)
    conv1(0)
    conv1(1)
    conv2(0)
    conv2(1)
    conv3(0)
    conv3(1)

    def last(z):
        p = []
        for dy in range(3):
            p.append(sum(q3[z + dz, dz * 48 + dy * 16:dz * 48 + dy * 16 + 16, :] for dz in range(3)))
        v = shifted_sum(*p)
        refined[0, z] = combined[0, z] + v[:B]
        refined[1, z] = combined[1, z] + v[B:]

    for z in range(B):
        last(z)

    for dz, dx in near:
        for p in range(1 if dz else Q):
            halo(dz, dx, p).wait_send()

    def drain(ref, sem):
        pltpu.make_async_copy(ref, ref, sem).wait()

    drain(gath.at[:, pl.ds(0, G - 1)], ag_send)
    drain(send1.at[:, :, pl.ds(0, Q * (CHUNK - ROWS))], a1_send)
    drain(send2.at[:, :, pl.ds(0, Q * (CHUNK - ROWS))], a2_send)
    drain(part.at[:, 0], sib_send)
    drain(rs_a.at[:, pl.ds(0, 7)], rs_send)


def hand_over(a_in, b_in, a_out, b_out, sem):
    copies = [pltpu.make_async_copy(a_in, a_out, sem.at[0]), pltpu.make_async_copy(b_in, b_out, sem.at[1])]
    for copy in copies:
        copy.start()
    for copy in copies:
        copy.wait()


def body(estimate, coil_maps, measured, line_mask, w_first, w_middle, w_last):
    tabs = [jnp.asarray(t) for t in tables()]
    measured = measured.reshape(2, 2, N * B, N)
    w_first = jnp.transpose(w_first, (0, 2, 1))
    operands = (estimate, coil_maps, measured, line_mask, w_first, w_middle, w_last, *tabs)
    vmem = pl.BlockSpec(memory_space=pltpu.VMEM)
    dma = pltpu.SemaphoreType.DMA
    block = jax.ShapeDtypeStruct((2, B, B, N), F32)
    results = pl.pallas_call(
        kernel,
        out_shape=(block, block),
        in_specs=[pl.BlockSpec(memory_space=pl.ANY)] * len(operands),
        out_specs=(vmem, vmem),
        scratch_shapes=[pltpu.VMEM(a.shape, a.dtype) for a in (
            estimate, coil_maps, measured, line_mask, w_first, w_middle, w_last,
            tabs[0], tabs[1], tabs[2], tabs[3], tabs[4], tabs[5])] + [
            pltpu.VMEM((Q, G, 2, ZQ, B, N), F32),
            pltpu.VMEM((2, 2, N * B, N), F32),
            pltpu.VMEM((2, 2, N * B, N), F32),
            pltpu.VMEM((2, 2, N * B, N), F32),
            pltpu.VMEM((2, 2, N * B, N), F32),
            pltpu.VMEM((Q, 2, 8, 2, ZQ, B, N), F32),
            pltpu.VMEM((Q, 8, 2, ZQ, B, N), F32),
            pltpu.VMEM((Q, 8, 2, ZQ, B, N), F32),
            pltpu.VMEM((1152, 512), BF16),
            pltpu.VMEM((192, 1152), BF16),
            pltpu.VMEM((288, 384), BF16),
            pltpu.VMEM((3, 2, 14, B, N), F32),
            pltpu.VMEM((48, 14 * N), BF16), pltpu.VMEM((48, 14 * N), BF16),
            pltpu.VMEM((384, 12 * N), BF16), pltpu.VMEM((384, 12 * N), BF16),
            pltpu.VMEM((320, 10 * N), BF16), pltpu.VMEM((320, 10 * N), BF16),
            pltpu.VMEM((10, 144, N), F32),
            dma((13,)), dma, dma((Q, G)), dma, dma((2, Q)), dma, dma((2, Q)),
            dma, dma((Q,)), dma, dma((Q,)), dma((14,)), dma((14,)),
        ],
        compiler_params=pltpu.CompilerParams(
            collective_id=0, has_side_effects=True, vmem_limit_bytes=56 * 2**20),
    )(*operands)
    anywhere = pl.BlockSpec(memory_space=pl.ANY)
    return pl.pallas_call(
        hand_over,
        out_shape=(block, block),
        in_specs=[anywhere] * 2,
        out_specs=(anywhere, anywhere),
        scratch_shapes=[dma((2,))],
    )(*results)


def solution(mesh):
    in_specs = (
        P(None, "slab", "coil", None),
        P("coil", None, "slab", None, None),
        P("coil", None, None, "slab", None),
        P(),
        P(),
        P(),
        P(),
    )
    out_specs = (P(None, "slab", "coil", None), P(None, "slab", "coil", None))
    return jax.shard_map(body, mesh=mesh, in_specs=in_specs, out_specs=out_specs, check_vma=False)
```

```python
import math

import jax
import jax.numpy as jnp
import ml_dtypes
import numpy as np
from jax import lax
from jax.experimental import pallas as pl
from jax.experimental.pallas import tpu as pltpu
from jax.sharding import PartitionSpec as P

MESH = pl.DeviceIdType.MESH
F32 = jnp.float32
BF16 = jnp.bfloat16
N = 128
B = 8
G = 16
ROWS = B
CHUNK = G * ROWS


def tables():
    k = np.arange(N)
    angle = 2.0 * math.pi * (np.outer(k, k) % N) / N
    c, s = np.cos(angle) / math.sqrt(N), np.sin(angle) / math.sqrt(N)
    fwd = np.block([[c, s], [-s, c]])
    inv = np.block([[c, -s], [s, c]])

    def pieces(m):
        hi = m.astype(np.float32).astype(ml_dtypes.bfloat16)
        lo = (m - hi.astype(np.float64)).astype(np.float32).astype(ml_dtypes.bfloat16)
        return [hi, hi, lo]

    order = np.arange(N).reshape(G, B).T.reshape(-1)
    order = np.concatenate([order, order + N])
    return [
        np.concatenate(pieces(fwd), 1),
        np.concatenate(pieces(inv), 1),
        np.concatenate(pieces(inv), 0),
        np.concatenate(pieces(fwd), 0),
        np.concatenate(pieces(fwd[:, order]), 1),
        np.concatenate(pieces(inv[order]), 1),
    ]


def split(x):
    hi = x.astype(BF16)
    lo = (x - hi.astype(F32)).astype(BF16)
    return hi, lo


def left(table, x):
    hi, lo = split(x)
    return jnp.dot(table, jnp.concatenate([hi, lo, hi], 0), preferred_element_type=F32)


def right(x, table):
    hi, lo = split(x)
    return jnp.dot(jnp.concatenate([hi, lo, hi], 1), table, preferred_element_type=F32)


def loop(count, fn):
    def step(i, carry):
        fn(i)
        return carry

    lax.fori_loop(0, count, step, 0)


def shifted_sum(p0, p1, p2):
    lane = lax.broadcasted_iota(jnp.int32, p0.shape, 1)
    down = jnp.where(lane == 0, 0.0, pltpu.roll(p0, 1, 1))
    up = jnp.where(lane == N - 1, 0.0, pltpu.roll(p2, N - 1, 1))
    return p1 + down + up


def build_weights(wf, wm, wl, w1, w2, w3, depth):
    lane = lax.broadcasted_iota(jnp.int32, (32, 512), 1)
    for dy in range(3):
        base = jnp.zeros((32, 512), F32)
        for dz in range(3):
            for dx in range(3):
                taps = jnp.transpose(jnp.concatenate([wf[depth(dz) * 9 + dx * 3 + dy], jnp.zeros((6, 32), F32)], 0))
                for c in range(2):
                    base = jnp.where(lane == dz * 48 + c * 24 + dx + 5, taps[:, c:c + 1], base)
        hi = base.astype(BF16).astype(F32)
        full = hi + pltpu.roll(hi, 144, 1) + pltpu.roll(base - hi, 288, 1)
        for xo in range(12):
            r = xo // 4 * 384 + dy * 128 + xo % 4 * 32
            w1[r:r + 32, :] = (pltpu.roll(full, xo, 1) if xo else full).astype(BF16)
    for dz in range(3):
        for dy in range(3):
            base = jnp.concatenate(
                [wm[depth(dz) * 9 + dx * 3 + dy] for dx in range(3)] + [jnp.zeros((32, 32), F32)], 1)
            for xo in range(2):
                hi, lo = split(pltpu.roll(base, 32, 1) if xo else base)
                r = (dy * 2 + xo) * 32
                for part, value in enumerate((hi, hi, lo)):
                    w2[r:r + 32, part * 384 + dz * 128:part * 384 + dz * 128 + 128] = value
    for dz in range(3):
        for dy in range(3):
            base = jnp.concatenate(
                [wl[depth(dz) * 9 + dx * 3 + dy] for dx in range(3)] + [jnp.zeros((2, 416), F32)], 1)
            both = jnp.concatenate([jnp.broadcast_to(base[o:o + 1], (8, 512)) for o in range(2)], 0)
            row = lax.broadcasted_iota(jnp.int32, (16, 512), 0) % 8
            moved = both
            for xo in range(1, 8):
                moved = jnp.where(row == xo, pltpu.roll(both, 32 * xo, 1), moved)
            hi, lo = split(moved[:, :384])
            r = dz * 48 + dy * 16
            w3[r:r + 16, :] = hi
            w3[144 + r:160 + r, :] = lo


def kernel(
    est_in, maps_in, meas_in, mask_in, wf_in, wm_in, wl_in, t0, t1, t2, t3, t4, t5,
    combined, refined,
    est, maps, meas, mask, wf, wm, wl, lf, li, rf, ri_, lzf, lzi,
    gath, send1, recv1, send2, recv2, part, sums,
    w1, w2, w3, big, f0h, f0l, f1h, f1l, f2h, f2l, q3,
    load_sem, ag_send, ag_recv, a1_send, a1_recv, a2_send, a2_recv,
    rs_send, rs_recv, halo_send, halo_recv,
):
    me_c = lax.axis_index("coil")
    me_s = lax.axis_index("slab")
    odd = lax.rem(me_s, 2)
    sign = 1 - 2 * odd

    def plane(t):
        return (B - 1) * odd + sign * t

    barrier = pltpu.get_barrier_semaphore()

    def near_id(dz, dx):
        return {"coil": lax.rem(me_c + dx + G, G), "slab": lax.rem(me_s + sign * dz + G, G)}

    def greet(target):
        pl.semaphore_signal(barrier, inc=1, device_id=target, device_id_type=MESH)

    def greet_lines(k):
        greet({"coil": lax.rem(me_c + k + 1, G)})
        greet({"slab": lax.rem(me_s + k + 1, G)})

    loop(G - 1, greet_lines)
    for dz in (-1, 1):
        for dx in (-1, 1):
            greet(near_id(dz, dx))

    pairs = [(est_in, est), (t0, lf), (maps_in, maps), (wf_in, wf), (wm_in, wm), (wl_in, wl), (t2, rf), (t4, lzf),
             (meas_in, meas), (mask_in, mask), (t5, lzi), (t3, ri_), (t1, li)]
    loads = [pltpu.make_async_copy(a, b, load_sem.at[i]) for i, (a, b) in enumerate(pairs)]
    for load in loads:
        load.start()
    pl.semaphore_wait(barrier, 2 * (G - 1) + 4)

    def gather_out(q):
        def out(k):
            pltpu.make_async_remote_copy(
                src_ref=est.at[:, q], dst_ref=gath.at[q, me_c], send_sem=ag_send, recv_sem=ag_recv.at[q],
                device_id={"coil": lax.rem(me_c + k + 1, G)}, device_id_type=MESH).start()

        loop(G - 1, out)
        gath[q, me_c] = est[:, q]

    def gather_in(q):
        ref = gath.at[q, pl.ds(0, G - 1)]
        pltpu.make_async_copy(ref, ref, ag_recv.at[q]).wait()

    def exchange(buf, dst, c, q, peer, send_sem, recv_sem, turned):
        at = q + lax.rem(peer, 2) * (B - 1 - 2 * q) if turned else q
        return pltpu.make_async_remote_copy(
            src_ref=buf.at[c, :, pl.ds(pl.multiple_of(at * CHUNK + peer * ROWS, ROWS), ROWS), :],
            dst_ref=dst.at[c, :, pl.ds(pl.multiple_of(at * CHUNK + me_s * ROWS, ROWS), ROWS), :],
            send_sem=send_sem, recv_sem=recv_sem.at[c, q],
            device_id={"slab": peer}, device_id_type=MESH)

    def exchange_out(buf, dst, c, q, send_sem, recv_sem, turned=False):
        def out(k):
            exchange(buf, dst, c, q, lax.rem(me_s + k + 1, G), send_sem, recv_sem, turned).start()

        loop(G - 1, out)
        at = plane(q) if turned else q
        own = pl.ds(pl.multiple_of(at * CHUNK + me_s * ROWS, ROWS), ROWS)
        for r in range(2):
            dst[c, r, own, :] = buf[c, r, own, :]

    def all_of(buf, c, q):
        return buf.at[c, :, pl.ds(pl.multiple_of(q * CHUNK, CHUNK), CHUNK - ROWS), :]

    def exchange_in(dst, c, q, recv_sem):
        ref = all_of(dst, c, q)
        pltpu.make_async_copy(ref, ref, recv_sem.at[c, q]).wait()

    def slab_plane(c, q):
        ir = gath[q, :, 0].reshape(N, N)
        ii = gath[q, :, 1].reshape(N, N)
        mr = maps[c, 0, q]
        mi = maps[c, 1, q]
        y = left(lf[...], jnp.concatenate([mr * ir - mi * ii, mr * ii + mi * ir], 0))
        for r in range(2):
            send1[c, r, pl.ds(pl.multiple_of(q * CHUNK, CHUNK), CHUNK), :] = y[r * N:(r + 1) * N]
        exchange_out(send1, recv1, c, q, a1_send, a1_recv)

    loads[0].wait()
    gather_out(0)
    gather_out(1)
    loads[1].wait()
    loads[2].wait()
    for q in range(B):
        gather_in(q)
        if q + 2 < B:
            gather_out(q + 2)
        slab_plane(0, q)
    loop(B, lambda q: slab_plane(1, q))

    for load in loads[3:]:
        load.wait()
    build_weights(wf, wm, wl, w1, w2, w3, lambda dz: 2 * odd + sign * dz)

    def pencils(c):
        loop(B, lambda q: exchange_in(recv1, c, q, a1_recv))

        def pair(kp):
            rows = []
            for j in range(2):
                rows.append(jnp.concatenate(
                    [recv1[c, r, pl.ds(2 * kp + j, N, stride=ROWS), :] for r in range(2)], 1))
            y = right(jnp.concatenate(rows, 0), rf[...])
            x = jnp.concatenate([
                jnp.concatenate([y[:N, :N], y[N:, :N]], 1),
                jnp.concatenate([y[:N, N:], y[N:, N:]], 1)], 0)
            x = left(lzf[...], x)
            w = jnp.where(mask[...] == 1, 0.5, 0.0)
            halves = []
            for r in range(2):
                pieces = []
                for j in range(2):
                    k = x[r * N:(r + 1) * N, j * N:(j + 1) * N]
                    m = meas[c, r, pl.ds(2 * kp + j, N, stride=B), :]
                    pieces.append(k - w * (k - m))
                halves.append(jnp.concatenate(pieces, 1))
            x = left(lzi[...], jnp.concatenate(halves, 0))
            y = jnp.concatenate([
                jnp.concatenate([x[:N, :N], x[N:, :N]], 1),
                jnp.concatenate([x[:N, N:], x[N:, N:]], 1)], 0)
            y = right(y, ri_[...])
            for j in range(2):
                for r in range(2):
                    send2[c, r, pl.ds(2 * kp + j, N, stride=ROWS), :] = y[j * N:(j + 1) * N, r * N:(r + 1) * N]

        loop(4, pair)
        loop(B, lambda p: exchange_out(send2, recv2, c, p, a2_send, a2_recv, True))

    loop(2, pencils)

    def coil_back(c, p):
        exchange_in(recv2, c, p, a2_recv)
        z = plane(p)
        at = pl.ds(pl.multiple_of(z * CHUNK, CHUNK), CHUNK)
        x = left(li[...], jnp.concatenate([recv2[c, 0, at, :], recv2[c, 1, at, :]], 0))
        br = x[:N]
        bi = x[N:]
        mr = maps[c, 0, z]
        mi = maps[c, 1, z]
        for r, v in enumerate((mr * br + mi * bi, mr * bi - mi * br)):
            v = v.reshape(G, B, N)
            part[p, :, r] = v if c == 0 else part[p, :, r] + v

    near = [(a, b) for a in (-1, 0, 1) for b in (-1, 0, 1) if (a, b) != (0, 0)]

    def halo(dz, dx, p=0):
        if dz:
            a, b, n = (3, 0, 3) if dz < 0 else (8 + 2 * p, 11 + 2 * p, 2 - p)
            i = dx + 1 + 3 * (dz > 0) + 3 * p
        else:
            a, b, n = 3 + p, 3 + p, 1
            i = 9 + 2 * p + (dx + 1) // 2
        return pltpu.make_async_remote_copy(
            src_ref=big.at[1, :, pl.ds(a, n)], dst_ref=big.at[1 - dx, :, pl.ds(b, n)],
            send_sem=halo_send.at[i], recv_sem=halo_recv.at[i],
            device_id=near_id(dz, dx), device_id_type=MESH)

    def spread(p):
        def out(k):
            target = lax.rem(me_c + k + 1, G)
            pltpu.make_async_remote_copy(
                src_ref=part.at[p, target], dst_ref=sums.at[p, me_c], send_sem=rs_send, recv_sem=rs_recv.at[p],
                device_id={"coil": target}, device_id_type=MESH).start()

        loop(G - 1, out)
        sums[p, me_c] = part[p, me_c]

    def total(p):
        ref = sums.at[p, pl.ds(0, G - 1)]
        pltpu.make_async_copy(ref, ref, rs_recv.at[p]).wait()
        value = sums[p, 0]
        for k in range(1, G):
            value = value + sums[p, k]
        big[1, :, 3 + p] = value
        if p == 7:
            for dx in (0, -1, 1):
                halo(1, dx, 1).start()
        halo(0, -1, p).start()
        halo(0, 1, p).start()
        if p in (2, 6):
            for dx in (0, -1, 1):
                halo(-1 if p == 2 else 1, dx).start()
        combined[:, plane(p)] = value

    low_c, high_c, edge = me_c == 0, me_c == G - 1, (me_s == 0) | (me_s == G - 1)

    def guard(v, *outside):
        for out, here in outside:
            if here:
                v = jnp.where(out, 0.0, v)
        return v

    def layer0(z):
        rows = []
        for c in range(2):
            for blk in range(3):
                row = 2 - z if z < 3 else 24 - z if z >= 11 else z
                rows.append(guard(big[blk, c, row], (low_c, blk == 0), (high_c, blk == 2), (edge, z < 3)))
        f0h[:, z * N:(z + 1) * N], f0l[:, z * N:(z + 1) * N] = split(jnp.concatenate(rows, 0))

    def window(hi, lo, i, rows):
        h = [hi[rows, (2 * i + dz) * N:(2 * i + dz + 2) * N] for dz in range(3)]
        l = [lo[rows, (2 * i + dz) * N:(2 * i + dz + 2) * N] for dz in range(3)]
        return jnp.concatenate(h + l + h, 0)

    def conv1(i):
        data = window(f0h, f0l, i, slice(0, 48))
        for g in range(3):
            y = jnp.dot(w1[g * 384:(g + 1) * 384, 0:432], data, preferred_element_type=F32)
            for j in range(2):
                z = 2 * i + j
                v = jnp.maximum(shifted_sum(*[y[d * 128:(d + 1) * 128, j * N:(j + 1) * N] for d in range(3)]), 0.0)
                v = guard(v, (edge, z < 2))
                v = jnp.concatenate([
                    guard(v[:64], (low_c, g == 0)), guard(v[64:], (high_c, g == 2))], 0)
                at = (slice(g * 128, (g + 1) * 128), slice(z * N, (z + 1) * N))
                f1h[at], f1l[at] = split(v)

    def conv2(i):
        for g in range(5):
            data = window(f1h, f1l, i, slice(g * 64, g * 64 + 128))
            y = jnp.dot(w2[...], data, preferred_element_type=F32)
            for j in range(2):
                z = 2 * i + j
                v = jnp.maximum(shifted_sum(*[y[d * 64:(d + 1) * 64, j * N:(j + 1) * N] for d in range(3)]), 0.0)
                v = guard(v, (edge, z < 1))
                v = jnp.concatenate([
                    guard(v[:32], (low_c, g == 0)), guard(v[32:], (high_c, g == 4))], 0)
                at = (slice(g * 64, (g + 1) * 64), slice(z * N, (z + 1) * N))
                f2h[at], f2l[at] = split(v)

    def conv3(i):
        at = slice(2 * i * N, (2 * i + 2) * N)
        y = jnp.dot(w3[:, 0:320], f2h[:, at], preferred_element_type=F32)
        y = y[:144] + y[144:] + jnp.dot(w3[0:144, 0:320], f2l[:, at], preferred_element_type=F32)
        q3[2 * i] = y[:, :N]
        q3[2 * i + 1] = y[:, N:]

    def sides_in(*quarters):
        for p in quarters:
            halo(0, -1, p).wait_recv()
            halo(0, 1, p).wait_recv()

    def ends_in(dz, p=0):
        for dx in (-1, 0, 1):
            halo(dz, dx, p).wait_recv()

    def layers(planes, firsts, seconds):
        for z in planes:
            layer0(z)
        for i in firsts:
            conv1(i)
        for i in seconds:
            conv2(i)
        for i in seconds:
            conv3(i)

    def last(z):
        p = []
        for dy in range(3):
            p.append(sum(q3[z + dz, dz * 48 + dy * 16:dz * 48 + dy * 16 + 16, :] for dz in range(3)))
        v = shifted_sum(*p)
        for c in range(2):
            refined[c, plane(z)] = big[1, c, 3 + z] + v[c * B:(c + 1) * B]

    loop(B, lambda p: coil_back(0, p))
    for p in range(B):
        coil_back(1, p)
        spread(p)
        if p > 1:
            total(p - 2)
    sides_in(0, 1, 2, 3)
    ends_in(-1)
    layers(range(7), (0, 1), ())
    total(6)
    layers((), (), (0,))
    sides_in(4, 5)
    layers((7, 8), (2,), (1,))
    total(7)
    sides_in(6)
    layers((9,), (3,), (2,))
    for z in range(4):
        last(z)
    ends_in(1)
    layers((12, 13), (), ())
    sides_in(7)
    ends_in(1, 1)
    layers((10, 11), (4, 5), (3, 4))
    for z in range(4, B):
        last(z)

    for dz, dx in near:
        for p in range({-1: 1, 0: B, 1: 2}[dz]):
            halo(dz, dx, p).wait_send()

    def drain(ref, sem):
        pltpu.make_async_copy(ref, ref, sem).wait()

    drain(gath.at[:, pl.ds(0, G - 1)], ag_send)
    drain(send1.at[:, :, pl.ds(0, B * (CHUNK - ROWS))], a1_send)
    drain(send2.at[:, :, pl.ds(0, B * (CHUNK - ROWS))], a2_send)
    drain(part.at[:, pl.ds(0, G - 1)], rs_send)


def hand_over(a_in, b_in, a_out, b_out):
    a_out[...] = a_in[...]
    b_out[...] = b_in[...]


def body(estimate, coil_maps, measured, line_mask, w_first, w_middle, w_last):
    tabs = [jnp.asarray(t) for t in tables()]
    measured = measured.reshape(2, 2, N * B, N)
    w_first = jnp.transpose(w_first, (0, 2, 1))
    operands = (estimate, coil_maps, measured, line_mask, w_first, w_middle, w_last, *tabs)
    vmem = pl.BlockSpec(memory_space=pltpu.VMEM)
    dma = pltpu.SemaphoreType.DMA
    block = jax.ShapeDtypeStruct((2, B, B, N), F32)
    results = pl.pallas_call(
        kernel,
        out_shape=(block, block),
        in_specs=[pl.BlockSpec(memory_space=pl.ANY)] * len(operands),
        out_specs=(vmem, vmem),
        scratch_shapes=[pltpu.VMEM(a.shape, a.dtype) for a in (
            estimate, coil_maps, measured, line_mask, w_first, w_middle, w_last,
            tabs[0], tabs[1], tabs[2], tabs[3], tabs[4], tabs[5])] + [
            pltpu.VMEM((B, G, 2, B, N), F32),
            pltpu.VMEM((2, 2, N * B, N), F32),
            pltpu.VMEM((2, 2, N * B, N), F32),
            pltpu.VMEM((2, 2, N * B, N), F32),
            pltpu.VMEM((2, 2, N * B, N), F32),
            pltpu.VMEM((B, G, 2, B, N), F32),
            pltpu.VMEM((B, G, 2, B, N), F32),
            pltpu.VMEM((1152, 512), BF16),
            pltpu.VMEM((192, 1152), BF16),
            pltpu.VMEM((288, 384), BF16),
            pltpu.VMEM((3, 2, 14, B, N), F32),
            pltpu.VMEM((48, 14 * N), BF16), pltpu.VMEM((48, 14 * N), BF16),
            pltpu.VMEM((384, 12 * N), BF16), pltpu.VMEM((384, 12 * N), BF16),
            pltpu.VMEM((320, 10 * N), BF16), pltpu.VMEM((320, 10 * N), BF16),
            pltpu.VMEM((10, 144, N), F32),
            dma((13,)), dma, dma((B,)), dma, dma((2, B)), dma, dma((2, B)), dma, dma((B,)), dma((25,)), dma((25,)),
        ],
        compiler_params=pltpu.CompilerParams(
            collective_id=0, has_side_effects=True, vmem_limit_bytes=56 * 2**20),
    )(*operands)
    return pl.pallas_call(
        hand_over,
        out_shape=(block, block),
        in_specs=[vmem] * 2,
        out_specs=(vmem, vmem),
    )(*results)


def solution(mesh):
    in_specs = (
        P(None, "slab", "coil", None),
        P("coil", None, "slab", None, None),
        P("coil", None, None, "slab", None),
        P(),
        P(),
        P(),
        P(),
    )
    out_specs = (P(None, "slab", "coil", None), P(None, "slab", "coil", None))
    return jax.shard_map(body, mesh=mesh, in_specs=in_specs, out_specs=out_specs, check_vma=False)
```

```python
import math

import jax
import jax.numpy as jnp
import ml_dtypes
import numpy as np
from jax import lax
from jax.experimental import pallas as pl
from jax.experimental.pallas import tpu as pltpu
from jax.sharding import PartitionSpec as P

MESH = pl.DeviceIdType.MESH
F32 = jnp.float32
BF16 = jnp.bfloat16
N = 128
B = 8
G = 16
ROWS = B
CHUNK = G * ROWS


def tables():
    k = np.arange(N)
    angle = 2.0 * math.pi * (np.outer(k, k) % N) / N
    c, s = np.cos(angle) / math.sqrt(N), np.sin(angle) / math.sqrt(N)
    fwd = np.block([[c, s], [-s, c]])
    inv = np.block([[c, -s], [s, c]])

    def pieces(m):
        hi = m.astype(np.float32).astype(ml_dtypes.bfloat16)
        lo = (m - hi.astype(np.float64)).astype(np.float32).astype(ml_dtypes.bfloat16)
        return [hi, hi, lo]

    order = np.arange(N).reshape(G, B).T.reshape(-1)
    order = np.concatenate([order, order + N])
    return [
        np.concatenate(pieces(fwd), 1),
        np.concatenate(pieces(inv), 1),
        np.concatenate(pieces(inv), 0),
        np.concatenate(pieces(fwd), 0),
        np.concatenate(pieces(fwd[:, order]), 1),
        np.concatenate(pieces(inv[order]), 1),
    ]


def split(x):
    hi = x.astype(BF16)
    lo = (x - hi.astype(F32)).astype(BF16)
    return hi, lo


def left(table, x):
    hi, lo = split(x)
    return jnp.dot(table, jnp.concatenate([hi, lo, hi], 0), preferred_element_type=F32)


def right(x, table):
    hi, lo = split(x)
    return jnp.dot(jnp.concatenate([hi, lo, hi], 1), table, preferred_element_type=F32)


def loop(count, fn):
    def step(i, carry):
        fn(i)
        return carry

    lax.fori_loop(0, count, step, 0)


def shifted_sum(p0, p1, p2):
    lane = lax.broadcasted_iota(jnp.int32, p0.shape, 1)
    down = jnp.where(lane == 0, 0.0, pltpu.roll(p0, 1, 1))
    up = jnp.where(lane == N - 1, 0.0, pltpu.roll(p2, N - 1, 1))
    return p1 + down + up


def build_weights(wf, wm, wl, w1, w2, w3):
    lane = lax.broadcasted_iota(jnp.int32, (32, 512), 1)
    for dy in range(3):
        base = jnp.zeros((32, 512), F32)
        for dz in range(3):
            for dx in range(3):
                taps = jnp.transpose(jnp.concatenate([wf[dz * 9 + dx * 3 + dy], jnp.zeros((6, 32), F32)], 0))
                for c in range(2):
                    base = jnp.where(lane == dz * 48 + c * 24 + dx + 5, taps[:, c:c + 1], base)
        hi = base.astype(BF16).astype(F32)
        full = hi + pltpu.roll(hi, 144, 1) + pltpu.roll(base - hi, 288, 1)
        for xo in range(12):
            r = xo // 4 * 384 + dy * 128 + xo % 4 * 32
            w1[r:r + 32, :] = (pltpu.roll(full, xo, 1) if xo else full).astype(BF16)
    for dz in range(3):
        for dy in range(3):
            base = jnp.concatenate(
                [wm[dz * 9 + dx * 3 + dy] for dx in range(3)] + [jnp.zeros((32, 32), F32)], 1)
            for xo in range(2):
                hi, lo = split(pltpu.roll(base, 32, 1) if xo else base)
                r = (dy * 2 + xo) * 32
                for part, value in enumerate((hi, hi, lo)):
                    w2[r:r + 32, part * 384 + dz * 128:part * 384 + dz * 128 + 128] = value
    for dz in range(3):
        for dy in range(3):
            base = jnp.concatenate(
                [wl[dz * 9 + dx * 3 + dy] for dx in range(3)] + [jnp.zeros((2, 416), F32)], 1)
            both = jnp.concatenate([jnp.broadcast_to(base[o:o + 1], (8, 512)) for o in range(2)], 0)
            row = lax.broadcasted_iota(jnp.int32, (16, 512), 0) % 8
            moved = both
            for xo in range(1, 8):
                moved = jnp.where(row == xo, pltpu.roll(both, 32 * xo, 1), moved)
            hi, lo = split(moved[:, :384])
            r = dz * 48 + dy * 16
            w3[r:r + 16, :] = hi
            w3[144 + r:160 + r, :] = lo


def kernel(
    est_in, maps_in, meas_in, mask_in, wf_in, wm_in, wl_in, t0, t1, t2, t3, t4, t5,
    combined, refined,
    est, maps, meas, mask, wf, wm, wl, lf, li, rf, ri_, lzf, lzi,
    gath, send1, recv1, send2, recv2, part, sums,
    w1, w2, w3, big, f0h, f0l, f1h, f1l, f2h, f2l, q3,
    load_sem, ag_send, ag_recv, a1_send, a1_recv, a2_send, a2_recv,
    rs_send, rs_recv, halo_send, halo_recv,
):
    me_c = lax.axis_index("coil")
    me_s = lax.axis_index("slab")

    def plane(p):
        return p // 2 + p % 2 * (B - 1 - p // 2 * 2)

    barrier = pltpu.get_barrier_semaphore()

    def near_id(dz, dx):
        return {"coil": lax.rem(me_c + dx + G, G), "slab": lax.rem(me_s + dz + G, G)}

    def far_first(k):
        return lax.rem(me_c + G // 2 + (k + 1) // 2 * (2 * lax.rem(k, 2) - 1) + G, G)

    def greet(target):
        pl.semaphore_signal(barrier, inc=1, device_id=target, device_id_type=MESH)

    def greet_lines(k):
        greet({"coil": lax.rem(me_c + k + 1, G)})
        greet({"slab": lax.rem(me_s + k + 1, G)})

    loop(G - 1, greet_lines)
    for dz in (-1, 1):
        for dx in (-1, 1):
            greet(near_id(dz, dx))

    pairs = [(est_in, est), (t0, lf), (maps_in, maps), (wf_in, wf), (wm_in, wm), (wl_in, wl), (t2, rf), (t4, lzf),
             (meas_in, meas), (mask_in, mask), (t5, lzi), (t3, ri_), (t1, li)]
    loads = [pltpu.make_async_copy(a, b, load_sem.at[i]) for i, (a, b) in enumerate(pairs)]
    for load in loads:
        load.start()
    pl.semaphore_wait(barrier, 2 * (G - 1) + 4)

    def gather_out(q):
        def out(k):
            pltpu.make_async_remote_copy(
                src_ref=est.at[:, q], dst_ref=gath.at[q, me_c], send_sem=ag_send, recv_sem=ag_recv.at[q],
                device_id={"coil": far_first(k)}, device_id_type=MESH).start()

        loop(G - 1, out)
        gath[q, me_c] = est[:, q]

    def gather_in(q):
        ref = gath.at[q, pl.ds(0, G - 1)]
        pltpu.make_async_copy(ref, ref, ag_recv.at[q]).wait()

    def exchange(buf, dst, c, q, peer, send_sem, recv_sem, turned):
        at = plane(q) if turned else q
        return pltpu.make_async_remote_copy(
            src_ref=buf.at[c, :, pl.ds(pl.multiple_of(at * CHUNK + peer * ROWS, ROWS), ROWS), :],
            dst_ref=dst.at[c, :, pl.ds(pl.multiple_of(at * CHUNK + me_s * ROWS, ROWS), ROWS), :],
            send_sem=send_sem, recv_sem=recv_sem.at[c, q],
            device_id={"slab": peer}, device_id_type=MESH)

    def exchange_out(buf, dst, c, q, send_sem, recv_sem, turned=False):
        def out(k):
            exchange(buf, dst, c, q, lax.rem(me_s + k + 1, G), send_sem, recv_sem, turned).start()

        loop(G - 1, out)
        at = plane(q) if turned else q
        own = pl.ds(pl.multiple_of(at * CHUNK + me_s * ROWS, ROWS), ROWS)
        for r in range(2):
            dst[c, r, own, :] = buf[c, r, own, :]

    def all_of(buf, c, q):
        return buf.at[c, :, pl.ds(pl.multiple_of(q * CHUNK, CHUNK), CHUNK - ROWS), :]

    def exchange_in(dst, c, q, recv_sem):
        ref = all_of(dst, c, q)
        pltpu.make_async_copy(ref, ref, recv_sem.at[c, q]).wait()

    def slab_plane(c, q):
        ir = gath[q, :, 0].reshape(N, N)
        ii = gath[q, :, 1].reshape(N, N)
        mr = maps[c, 0, q]
        mi = maps[c, 1, q]
        y = left(lf[...], jnp.concatenate([mr * ir - mi * ii, mr * ii + mi * ir], 0))
        for r in range(2):
            send1[c, r, pl.ds(pl.multiple_of(q * CHUNK, CHUNK), CHUNK), :] = y[r * N:(r + 1) * N]
        exchange_out(send1, recv1, c, q, a1_send, a1_recv)

    loads[0].wait()
    for q in range(3):
        gather_out(q)
    loads[1].wait()
    loads[2].wait()
    for q in range(B):
        gather_in(q)
        if q + 3 < B:
            gather_out(q + 3)
        slab_plane(0, q)
        if q < 2:
            slab_plane(1, q)
    loop(B - 2, lambda q: slab_plane(1, q + 2))

    for load in loads[3:]:
        load.wait()
    build_weights(wf, wm, wl, w1, w2, w3)

    def pencils(c):
        loop(B, lambda q: exchange_in(recv1, c, q, a1_recv))

        def pair(kp):
            rows = []
            for j in range(2):
                rows.append(jnp.concatenate(
                    [recv1[c, r, pl.ds(2 * kp + j, N, stride=ROWS), :] for r in range(2)], 1))
            y = right(jnp.concatenate(rows, 0), rf[...])
            x = jnp.concatenate([
                jnp.concatenate([y[:N, :N], y[N:, :N]], 1),
                jnp.concatenate([y[:N, N:], y[N:, N:]], 1)], 0)
            x = left(lzf[...], x)
            w = jnp.where(mask[...] == 1, 0.5, 0.0)
            halves = []
            for r in range(2):
                pieces = []
                for j in range(2):
                    k = x[r * N:(r + 1) * N, j * N:(j + 1) * N]
                    m = meas[c, r, pl.ds(2 * kp + j, N, stride=B), :]
                    pieces.append(k - w * (k - m))
                halves.append(jnp.concatenate(pieces, 1))
            x = left(lzi[...], jnp.concatenate(halves, 0))
            y = jnp.concatenate([
                jnp.concatenate([x[:N, :N], x[N:, :N]], 1),
                jnp.concatenate([x[:N, N:], x[N:, N:]], 1)], 0)
            y = right(y, ri_[...])
            for j in range(2):
                for r in range(2):
                    send2[c, r, pl.ds(2 * kp + j, N, stride=ROWS), :] = y[j * N:(j + 1) * N, r * N:(r + 1) * N]

        loop(4, pair)
        loop(B, lambda p: exchange_out(send2, recv2, c, p, a2_send, a2_recv, True))

    loop(2, pencils)

    def coil_back(c, p):
        exchange_in(recv2, c, p, a2_recv)
        z = plane(p)
        at = pl.ds(pl.multiple_of(z * CHUNK, CHUNK), CHUNK)
        x = left(li[...], jnp.concatenate([recv2[c, 0, at, :], recv2[c, 1, at, :]], 0))
        br = x[:N]
        bi = x[N:]
        mr = maps[c, 0, z]
        mi = maps[c, 1, z]
        for r, v in enumerate((mr * br + mi * bi, mr * bi - mi * br)):
            v = v.reshape(G, B, N)
            part[p, :, r] = v if c == 0 else part[p, :, r] + v

    near = [(a, b) for a in (-1, 0, 1) for b in (-1, 0, 1) if (a, b) != (0, 0)]

    def halo(dz, dx, p=0):
        if dz:
            a, b, n = (3, 11, 3) if dz < 0 else (8, 0, 3)
            i = dx + 1 + 3 * (dz > 0)
        else:
            a, b, n = 3 + plane(p), 3 + plane(p), 1
            i = 6 + 2 * p + (dx + 1) // 2
        return pltpu.make_async_remote_copy(
            src_ref=big.at[1, :, pl.ds(a, n)], dst_ref=big.at[1 - dx, :, pl.ds(b, n)],
            send_sem=halo_send.at[i], recv_sem=halo_recv.at[i],
            device_id=near_id(dz, dx), device_id_type=MESH)

    def spread(p):
        def out(k):
            target = far_first(k)
            pltpu.make_async_remote_copy(
                src_ref=part.at[p, target], dst_ref=sums.at[p, me_c], send_sem=rs_send, recv_sem=rs_recv.at[p],
                device_id={"coil": target}, device_id_type=MESH).start()

        loop(G - 1, out)
        sums[p, me_c] = part[p, me_c]

    def total(p):
        ref = sums.at[p, pl.ds(0, G - 1)]
        pltpu.make_async_copy(ref, ref, rs_recv.at[p]).wait()
        value = sums[p, 0]
        for k in range(1, G):
            value = value + sums[p, k]
        big[1, :, 3 + plane(p)] = value
        halo(0, -1, p).start()
        halo(0, 1, p).start()
        if p in (4, 5):
            for dx in (0, -1, 1):
                halo(2 * p - 9, dx).start()
        combined[:, plane(p)] = value

    low_c, high_c, low_s, high_s = me_c == 0, me_c == G - 1, me_s == 0, me_s == G - 1

    def guard(v, *outside):
        for out, here in outside:
            if here:
                v = jnp.where(out, 0.0, v)
        return v

    def layer0(z, alone=False):
        rows = []
        for c in range(2):
            for blk in range(3):
                if alone and blk != 1:
                    rows.append(jnp.zeros((B, N), F32))
                    continue
                rows.append(guard(
                    big[blk, c, z], (low_c, blk == 0), (high_c, blk == 2), (low_s, z < 3), (high_s, z >= 11)))
        f0h[:, z * N:(z + 1) * N], f0l[:, z * N:(z + 1) * N] = split(jnp.concatenate(rows, 0))

    def window(hi, lo, i, rows):
        h = [hi[rows, (2 * i + dz) * N:(2 * i + dz + 2) * N] for dz in range(3)]
        l = [lo[rows, (2 * i + dz) * N:(2 * i + dz + 2) * N] for dz in range(3)]
        return jnp.concatenate(h + l + h, 0)

    def conv1(i, groups=(0, 1, 2)):
        data = window(f0h, f0l, i, slice(0, 48))
        for g in groups:
            y = jnp.dot(w1[g * 384:(g + 1) * 384, 0:432], data, preferred_element_type=F32)
            for j in range(2):
                z = 2 * i + j
                v = jnp.maximum(shifted_sum(*[y[d * 128:(d + 1) * 128, j * N:(j + 1) * N] for d in range(3)]), 0.0)
                v = guard(v, (low_s, z < 2), (high_s, z >= 10))
                v = jnp.concatenate([
                    guard(v[:64], (low_c, g == 0)), guard(v[64:], (high_c, g == 2))], 0)
                at = (slice(g * 128, (g + 1) * 128), slice(z * N, (z + 1) * N))
                f1h[at], f1l[at] = split(v)

    def conv2(i, groups=(0, 1, 2, 3, 4)):
        for g in groups:
            data = window(f1h, f1l, i, slice(g * 64, g * 64 + 128))
            y = jnp.dot(w2[...], data, preferred_element_type=F32)
            for j in range(2):
                z = 2 * i + j
                v = jnp.maximum(shifted_sum(*[y[d * 64:(d + 1) * 64, j * N:(j + 1) * N] for d in range(3)]), 0.0)
                v = guard(v, (low_s, z < 1), (high_s, z >= 9))
                v = jnp.concatenate([
                    guard(v[:32], (low_c, g == 0)), guard(v[32:], (high_c, g == 4))], 0)
                at = (slice(g * 64, (g + 1) * 64), slice(z * N, (z + 1) * N))
                f2h[at], f2l[at] = split(v)

    def conv3(i):
        at = slice(2 * i * N, (2 * i + 2) * N)
        y = jnp.dot(w3[:, 0:320], f2h[:, at], preferred_element_type=F32)
        y = y[:144] + y[144:] + jnp.dot(w3[0:144, 0:320], f2l[:, at], preferred_element_type=F32)
        q3[2 * i] = y[:, :N]
        q3[2 * i + 1] = y[:, N:]

    def sides_in(*quarters):
        for p in quarters:
            halo(0, -1, p).wait_recv()
            halo(0, 1, p).wait_recv()

    def ends_in(dz):
        for dx in (-1, 0, 1):
            halo(dz, dx).wait_recv()

    def layers(planes, firsts, seconds):
        for z in planes:
            layer0(z)
        for i in firsts:
            conv1(i)
        for i in seconds:
            conv2(i)
        for i in seconds:
            conv3(i)

    def last(z):
        p = []
        for dy in range(3):
            p.append(sum(q3[z + dz, dz * 48 + dy * 16:dz * 48 + dy * 16 + 16, :] for dz in range(3)))
        v = shifted_sum(*p)
        for c in range(2):
            refined[c, z] = big[1, c, 3 + z] + v[c * B:(c + 1) * B]

    loop(B, lambda p: coil_back(0, p))
    for p in range(B):
        coil_back(1, p)
        spread(p)
        if p > 1:
            total(p - 2)
    sides_in(0, 1, 2, 3, 4)
    ends_in(-1)
    layers((3, 4, 5, 9, 10, 11, 12, 13), (5,), ())
    total(6)
    sides_in(5)
    layers((8,), (4,), (4,))
    total(7)
    ends_in(1)
    layers((0, 1, 2), (0, 1), (0,))
    sides_in(6)
    layer0(6)
    layer0(7, True)
    conv1(2, (1,))
    conv1(3, (1,))
    for i in (1, 2, 3):
        conv2(i, (2,))

    def drain(ref, sem):
        pltpu.make_async_copy(ref, ref, sem).wait()

    drain(gath.at[:, pl.ds(0, G - 1)], ag_send)
    drain(send1.at[:, :, pl.ds(0, B * (CHUNK - ROWS))], a1_send)
    drain(send2.at[:, :, pl.ds(0, B * (CHUNK - ROWS))], a2_send)
    drain(part.at[:, pl.ds(0, G - 1)], rs_send)
    for dz, dx in near:
        for p in range(1 if dz else B):
            halo(dz, dx, p).wait_send()
    sides_in(7)
    layer0(7)
    conv1(2, (0, 2))
    conv1(3, (0, 2))
    for i in (1, 2, 3):
        conv2(i, (0, 1, 3, 4))
    for i in (1, 2, 3):
        conv3(i)
    for z in range(B):
        last(z)


def hand_over(a_in, b_in, a_out, b_out):
    a_out[...] = a_in[...]
    b_out[...] = b_in[...]


def body(estimate, coil_maps, measured, line_mask, w_first, w_middle, w_last):
    tabs = [jnp.asarray(t) for t in tables()]
    measured = measured.reshape(2, 2, N * B, N)
    w_first = jnp.transpose(w_first, (0, 2, 1))
    operands = (estimate, coil_maps, measured, line_mask, w_first, w_middle, w_last, *tabs)
    vmem = pl.BlockSpec(memory_space=pltpu.VMEM)
    dma = pltpu.SemaphoreType.DMA
    block = jax.ShapeDtypeStruct((2, B, B, N), F32)
    results = pl.pallas_call(
        kernel,
        out_shape=(block, block),
        in_specs=[pl.BlockSpec(memory_space=pl.ANY)] * len(operands),
        out_specs=(vmem, vmem),
        scratch_shapes=[pltpu.VMEM(a.shape, a.dtype) for a in (
            estimate, coil_maps, measured, line_mask, w_first, w_middle, w_last,
            tabs[0], tabs[1], tabs[2], tabs[3], tabs[4], tabs[5])] + [
            pltpu.VMEM((B, G, 2, B, N), F32),
            pltpu.VMEM((2, 2, N * B, N), F32),
            pltpu.VMEM((2, 2, N * B, N), F32),
            pltpu.VMEM((2, 2, N * B, N), F32),
            pltpu.VMEM((2, 2, N * B, N), F32),
            pltpu.VMEM((B, G, 2, B, N), F32),
            pltpu.VMEM((B, G, 2, B, N), F32),
            pltpu.VMEM((1152, 512), BF16),
            pltpu.VMEM((192, 1152), BF16),
            pltpu.VMEM((288, 384), BF16),
            pltpu.VMEM((3, 2, 14, B, N), F32),
            pltpu.VMEM((48, 14 * N), BF16), pltpu.VMEM((48, 14 * N), BF16),
            pltpu.VMEM((384, 12 * N), BF16), pltpu.VMEM((384, 12 * N), BF16),
            pltpu.VMEM((320, 10 * N), BF16), pltpu.VMEM((320, 10 * N), BF16),
            pltpu.VMEM((10, 144, N), F32),
            dma((13,)), dma, dma((B,)), dma, dma((2, B)), dma, dma((2, B)), dma, dma((B,)), dma((22,)), dma((22,)),
        ],
        compiler_params=pltpu.CompilerParams(
            collective_id=0, has_side_effects=True, vmem_limit_bytes=56 * 2**20),
    )(*operands)
    return pl.pallas_call(
        hand_over,
        out_shape=(block, block),
        in_specs=[vmem] * 2,
        out_specs=(vmem, vmem),
    )(*results)


def solution(mesh):
    in_specs = (
        P(None, "slab", "coil", None),
        P("coil", None, "slab", None, None),
        P("coil", None, None, "slab", None),
        P(),
        P(),
        P(),
        P(),
    )
    out_specs = (P(None, "slab", "coil", None), P(None, "slab", "coil", None))
    return jax.shard_map(body, mesh=mesh, in_specs=in_specs, out_specs=out_specs, check_vma=False)
```

```python
import math

import jax
import jax.numpy as jnp
import ml_dtypes
import numpy as np
from jax import lax
from jax.experimental import pallas as pl
from jax.experimental.pallas import tpu as pltpu
from jax.sharding import PartitionSpec as P

MESH = pl.DeviceIdType.MESH
F32 = jnp.float32
BF16 = jnp.bfloat16
N = 128
B = 8
G = 16
ROWS = B
CHUNK = G * ROWS


def tables():
    k = np.arange(N)
    angle = 2.0 * math.pi * (np.outer(k, k) % N) / N
    c, s = np.cos(angle) / math.sqrt(N), np.sin(angle) / math.sqrt(N)
    fwd = np.block([[c, s], [-s, c]])
    inv = np.block([[c, -s], [s, c]])

    def pieces(m):
        hi = m.astype(np.float32).astype(ml_dtypes.bfloat16)
        lo = (m - hi.astype(np.float64)).astype(np.float32).astype(ml_dtypes.bfloat16)
        return [hi, hi, lo]

    order = np.arange(N).reshape(G, B).T.reshape(-1)
    order = np.concatenate([order, order + N])
    return [
        np.concatenate(pieces(fwd), 1),
        np.concatenate(pieces(inv), 1),
        np.concatenate(pieces(inv), 0),
        np.concatenate(pieces(fwd), 0),
        np.concatenate(pieces(fwd[:, order]), 1),
        np.concatenate(pieces(inv[order]), 1),
    ]


def split(x):
    hi = x.astype(BF16)
    lo = (x - hi.astype(F32)).astype(BF16)
    return hi, lo


def left(table, x):
    hi, lo = split(x)
    return jnp.dot(table, jnp.concatenate([hi, lo, hi], 0), preferred_element_type=F32)


def right(x, table):
    hi, lo = split(x)
    return jnp.dot(jnp.concatenate([hi, lo, hi], 1), table, preferred_element_type=F32)


def loop(count, fn):
    def step(i, carry):
        fn(i)
        return carry

    lax.fori_loop(0, count, step, 0)


def shifted_sum(p0, p1, p2):
    lane = lax.broadcasted_iota(jnp.int32, p0.shape, 1)
    down = jnp.where(lane == 0, 0.0, pltpu.roll(p0, 1, 1))
    up = jnp.where(lane == N - 1, 0.0, pltpu.roll(p2, N - 1, 1))
    return p1 + down + up


def build_weights(wf, wm, wl, w1, w2, w3):
    lane = lax.broadcasted_iota(jnp.int32, (32, 512), 1)
    for dy in range(3):
        base = jnp.zeros((32, 512), F32)
        for dz in range(3):
            for dx in range(3):
                taps = jnp.transpose(jnp.concatenate([wf[dz * 9 + dx * 3 + dy], jnp.zeros((6, 32), F32)], 0))
                for c in range(2):
                    base = jnp.where(lane == dz * 48 + c * 24 + dx + 5, taps[:, c:c + 1], base)
        hi = base.astype(BF16).astype(F32)
        full = hi + pltpu.roll(hi, 144, 1) + pltpu.roll(base - hi, 288, 1)
        for xo in range(12):
            r = xo // 4 * 384 + dy * 128 + xo % 4 * 32
            w1[r:r + 32, :] = (pltpu.roll(full, xo, 1) if xo else full).astype(BF16)
    for dz in range(3):
        for dy in range(3):
            base = jnp.concatenate(
                [wm[dz * 9 + dx * 3 + dy] for dx in range(3)] + [jnp.zeros((32, 32), F32)], 1)
            for xo in range(2):
                hi, lo = split(pltpu.roll(base, 32, 1) if xo else base)
                r = (dy * 2 + xo) * 32
                for part, value in enumerate((hi, hi, lo)):
                    w2[r:r + 32, part * 384 + dz * 128:part * 384 + dz * 128 + 128] = value
    for dz in range(3):
        for dy in range(3):
            base = jnp.concatenate(
                [wl[dz * 9 + dx * 3 + dy] for dx in range(3)] + [jnp.zeros((2, 416), F32)], 1)
            both = jnp.concatenate([jnp.broadcast_to(base[o:o + 1], (8, 512)) for o in range(2)], 0)
            row = lax.broadcasted_iota(jnp.int32, (16, 512), 0) % 8
            moved = both
            for xo in range(1, 8):
                moved = jnp.where(row == xo, pltpu.roll(both, 32 * xo, 1), moved)
            hi, lo = split(moved[:, :384])
            r = dz * 48 + dy * 16
            w3[r:r + 16, :] = hi
            w3[144 + r:160 + r, :] = lo


def kernel(
    est_in, maps_in, meas_in, mask_in, wf_in, wm_in, wl_in, t0, t1, t2, t3, t4, t5,
    combined, refined,
    est, maps, meas, mask, wf, wm, wl, lf, li, rf, ri_, lzf, lzi,
    gath, send1, recv1, send2, recv2, part, sums,
    w1, w2, w3, big, f0h, f0l, f1h, f1l, f2h, f2l, q3,
    load_sem, ag_send, ag_recv, a1_send, a1_recv, a2_send, a2_recv,
    rs_send, rs_recv, halo_send, halo_recv,
):
    me_c = lax.axis_index("coil")
    me_s = lax.axis_index("slab")

    def plane(p):
        return p // 2 + p % 2 * (B - 1 - p // 2 * 2)

    barrier = pltpu.get_barrier_semaphore()

    def near_id(dz, dx):
        return {"coil": lax.rem(me_c + dx + G, G), "slab": lax.rem(me_s + dz + G, G)}

    def far_first(k):
        return lax.rem(me_c + G // 2 + (k + 1) // 2 * (2 * lax.rem(k, 2) - 1) + G, G)

    def greet(target):
        pl.semaphore_signal(barrier, inc=1, device_id=target, device_id_type=MESH)

    def greet_lines(k):
        greet({"coil": lax.rem(me_c + k + 1, G)})
        greet({"slab": lax.rem(me_s + k + 1, G)})

    loop(G - 1, greet_lines)
    for dz in (-1, 1):
        for dx in (-1, 1):
            greet(near_id(dz, dx))

    pairs = [(est_in, est), (t0, lf), (maps_in, maps), (wf_in, wf), (wm_in, wm), (wl_in, wl), (t2, rf), (t4, lzf),
             (meas_in, meas), (mask_in, mask), (t5, lzi), (t3, ri_), (t1, li)]
    loads = [pltpu.make_async_copy(a, b, load_sem.at[i]) for i, (a, b) in enumerate(pairs)]
    for load in loads:
        load.start()
    pl.semaphore_wait(barrier, 2 * (G - 1) + 4)

    def gather_out(q):
        def out(k):
            pltpu.make_async_remote_copy(
                src_ref=est.at[:, q], dst_ref=gath.at[q, me_c], send_sem=ag_send, recv_sem=ag_recv.at[q],
                device_id={"coil": far_first(k)}, device_id_type=MESH).start()

        loop(G - 1, out)
        gath[q, me_c] = est[:, q]

    def gather_in(q):
        ref = gath.at[q, pl.ds(0, G - 1)]
        pltpu.make_async_copy(ref, ref, ag_recv.at[q]).wait()

    def exchange(buf, dst, c, q, peer, send_sem, recv_sem, turned):
        at = plane(q) if turned else q
        return pltpu.make_async_remote_copy(
            src_ref=buf.at[c, :, pl.ds(pl.multiple_of(at * CHUNK + peer * ROWS, ROWS), ROWS), :],
            dst_ref=dst.at[c, :, pl.ds(pl.multiple_of(at * CHUNK + me_s * ROWS, ROWS), ROWS), :],
            send_sem=send_sem, recv_sem=recv_sem.at[c, q],
            device_id={"slab": peer}, device_id_type=MESH)

    def exchange_out(buf, dst, c, q, send_sem, recv_sem, turned=False):
        def out(k):
            exchange(buf, dst, c, q, lax.rem(me_s + k + 1, G), send_sem, recv_sem, turned).start()

        loop(G - 1, out)
        at = plane(q) if turned else q
        own = pl.ds(pl.multiple_of(at * CHUNK + me_s * ROWS, ROWS), ROWS)
        for r in range(2):
            dst[c, r, own, :] = buf[c, r, own, :]

    def all_of(buf, c, q):
        return buf.at[c, :, pl.ds(pl.multiple_of(q * CHUNK, CHUNK), CHUNK - ROWS), :]

    def exchange_in(dst, c, q, recv_sem):
        ref = all_of(dst, c, q)
        pltpu.make_async_copy(ref, ref, recv_sem.at[c, q]).wait()

    def slab_plane(c, q):
        ir = gath[q, :, 0].reshape(N, N)
        ii = gath[q, :, 1].reshape(N, N)
        mr = maps[c, 0, q]
        mi = maps[c, 1, q]
        y = left(lf[...], jnp.concatenate([mr * ir - mi * ii, mr * ii + mi * ir], 0))
        for r in range(2):
            send1[c, r, pl.ds(pl.multiple_of(q * CHUNK, CHUNK), CHUNK), :] = y[r * N:(r + 1) * N]
        exchange_out(send1, recv1, c, q, a1_send, a1_recv)

    loads[0].wait()
    for q in range(3):
        gather_out(q)
    loads[1].wait()
    loads[2].wait()
    for q in range(B):
        gather_in(q)
        if q + 3 < B:
            gather_out(q + 3)
        slab_plane(0, q)
        if q < 2:
            slab_plane(1, q)
    loop(B - 2, lambda q: slab_plane(1, q + 2))

    for load in loads[3:]:
        load.wait()
    build_weights(wf, wm, wl, w1, w2, w3)

    def pencils(c):
        loop(B, lambda q: exchange_in(recv1, c, q, a1_recv))

        def pair(kp):
            rows = []
            for j in range(2):
                rows.append(jnp.concatenate(
                    [recv1[c, r, pl.ds(2 * kp + j, N, stride=ROWS), :] for r in range(2)], 1))
            y = right(jnp.concatenate(rows, 0), rf[...])
            x = jnp.concatenate([
                jnp.concatenate([y[:N, :N], y[N:, :N]], 1),
                jnp.concatenate([y[:N, N:], y[N:, N:]], 1)], 0)
            x = left(lzf[...], x)
            w = jnp.where(mask[...] == 1, 0.5, 0.0)
            halves = []
            for r in range(2):
                pieces = []
                for j in range(2):
                    k = x[r * N:(r + 1) * N, j * N:(j + 1) * N]
                    m = meas[c, r, pl.ds(2 * kp + j, N, stride=B), :]
                    pieces.append(k - w * (k - m))
                halves.append(jnp.concatenate(pieces, 1))
            x = left(lzi[...], jnp.concatenate(halves, 0))
            y = jnp.concatenate([
                jnp.concatenate([x[:N, :N], x[N:, :N]], 1),
                jnp.concatenate([x[:N, N:], x[N:, N:]], 1)], 0)
            y = right(y, ri_[...])
            for j in range(2):
                for r in range(2):
                    send2[c, r, pl.ds(2 * kp + j, N, stride=ROWS), :] = y[j * N:(j + 1) * N, r * N:(r + 1) * N]

        loop(4, pair)
        loop(B, lambda p: exchange_out(send2, recv2, c, p, a2_send, a2_recv, True))

    loop(2, pencils)

    def coil_back(c, p):
        exchange_in(recv2, c, p, a2_recv)
        z = plane(p)
        at = pl.ds(pl.multiple_of(z * CHUNK, CHUNK), CHUNK)
        x = left(li[...], jnp.concatenate([recv2[c, 0, at, :], recv2[c, 1, at, :]], 0))
        br = x[:N]
        bi = x[N:]
        mr = maps[c, 0, z]
        mi = maps[c, 1, z]
        for r, v in enumerate((mr * br + mi * bi, mr * bi - mi * br)):
            v = v.reshape(G, B, N)
            part[p, :, r] = v if c == 0 else part[p, :, r] + v

    near = [(a, b) for a in (-1, 0, 1) for b in (-1, 0, 1) if (a, b) != (0, 0)]

    def halo(dz, dx, p=0):
        if dz:
            a, b, n = (3, 11, 3) if dz < 0 else (8, 0, 3)
            i = dx + 1 + 3 * (dz > 0)
        else:
            a, b, n = 3 + plane(p), 3 + plane(p), 1
            i = 6 + 2 * p + (dx + 1) // 2
        return pltpu.make_async_remote_copy(
            src_ref=big.at[1, :, pl.ds(a, n)], dst_ref=big.at[1 - dx, :, pl.ds(b, n)],
            send_sem=halo_send.at[i], recv_sem=halo_recv.at[i],
            device_id=near_id(dz, dx), device_id_type=MESH)

    def spread(p):
        def out(k):
            target = far_first(k)
            pltpu.make_async_remote_copy(
                src_ref=part.at[p, target], dst_ref=sums.at[p, me_c], send_sem=rs_send, recv_sem=rs_recv.at[p],
                device_id={"coil": target}, device_id_type=MESH).start()

        loop(G - 1, out)
        sums[p, me_c] = part[p, me_c]

    def total(p):
        ref = sums.at[p, pl.ds(0, G - 1)]
        pltpu.make_async_copy(ref, ref, rs_recv.at[p]).wait()
        value = sums[p, 0]
        for k in range(1, G):
            value = value + sums[p, k]
        big[1, :, 3 + plane(p)] = value
        halo(0, -1, p).start()
        halo(0, 1, p).start()
        if p in (4, 5):
            for dx in (0, -1, 1):
                halo(2 * p - 9, dx).start()
        combined[:, plane(p)] = value

    low_c, high_c, low_s, high_s = me_c == 0, me_c == G - 1, me_s == 0, me_s == G - 1

    def guard(v, *outside):
        for out, here in outside:
            if here:
                v = jnp.where(out, 0.0, v)
        return v

    def layer0(z, alone=False):
        rows = []
        for c in range(2):
            for blk in range(3):
                if alone and blk != 1:
                    rows.append(jnp.zeros((B, N), F32))
                    continue
                rows.append(guard(
                    big[blk, c, z], (low_c, blk == 0), (high_c, blk == 2), (low_s, z < 3), (high_s, z >= 11)))
        f0h[:, z * N:(z + 1) * N], f0l[:, z * N:(z + 1) * N] = split(jnp.concatenate(rows, 0))

    def window(hi, lo, i, rows):
        h = [hi[rows, (2 * i + dz) * N:(2 * i + dz + 2) * N] for dz in range(3)]
        l = [lo[rows, (2 * i + dz) * N:(2 * i + dz + 2) * N] for dz in range(3)]
        return jnp.concatenate(h + l + h, 0)

    def conv1(i, groups=(0, 1, 2)):
        data = window(f0h, f0l, i, slice(0, 48))
        for g in groups:
            y = jnp.dot(w1[g * 384:(g + 1) * 384, 0:432], data, preferred_element_type=F32)
            for j in range(2):
                z = 2 * i + j
                v = jnp.maximum(shifted_sum(*[y[d * 128:(d + 1) * 128, j * N:(j + 1) * N] for d in range(3)]), 0.0)
                v = guard(v, (low_s, z < 2), (high_s, z >= 10))
                v = jnp.concatenate([
                    guard(v[:64], (low_c, g == 0)), guard(v[64:], (high_c, g == 2))], 0)
                at = (slice(g * 128, (g + 1) * 128), slice(z * N, (z + 1) * N))
                f1h[at], f1l[at] = split(v)

    def conv2(i, groups=(0, 1, 2, 3, 4)):
        for g in groups:
            data = window(f1h, f1l, i, slice(g * 64, g * 64 + 128))
            y = jnp.dot(w2[...], data, preferred_element_type=F32)
            for j in range(2):
                z = 2 * i + j
                v = jnp.maximum(shifted_sum(*[y[d * 64:(d + 1) * 64, j * N:(j + 1) * N] for d in range(3)]), 0.0)
                v = guard(v, (low_s, z < 1), (high_s, z >= 9))
                v = jnp.concatenate([
                    guard(v[:32], (low_c, g == 0)), guard(v[32:], (high_c, g == 4))], 0)
                at = (slice(g * 64, (g + 1) * 64), slice(z * N, (z + 1) * N))
                f2h[at], f2l[at] = split(v)

    def conv3(i):
        at = slice(2 * i * N, (2 * i + 2) * N)
        y = jnp.dot(w3[:, 0:320], f2h[:, at], preferred_element_type=F32)
        y = y[:144] + y[144:] + jnp.dot(w3[0:144, 0:320], f2l[:, at], preferred_element_type=F32)
        q3[2 * i] = y[:, :N]
        q3[2 * i + 1] = y[:, N:]

    def sides_in(*quarters):
        for p in quarters:
            halo(0, -1, p).wait_recv()
            halo(0, 1, p).wait_recv()

    def ends_in(dz):
        for dx in (-1, 0, 1):
            halo(dz, dx).wait_recv()

    def layers(planes, firsts, seconds):
        for z in planes:
            layer0(z)
        for i in firsts:
            conv1(i)
        for i in seconds:
            conv2(i)
        for i in seconds:
            conv3(i)

    def last(z):
        p = []
        for dy in range(3):
            p.append(sum(q3[z + dz, dz * 48 + dy * 16:dz * 48 + dy * 16 + 16, :] for dz in range(3)))
        v = shifted_sum(*p)
        for c in range(2):
            refined[c, z] = big[1, c, 3 + z] + v[c * B:(c + 1) * B]

    loop(B, lambda p: coil_back(0, p))
    for p in range(B):
        coil_back(1, p)
        spread(p)
        if p > 1:
            total(p - 2)
    sides_in(0, 1, 2, 3, 4)
    ends_in(-1)
    layers((3, 4, 5, 9, 10, 11, 12, 13), (5,), ())
    total(6)
    sides_in(5)
    layers((8,), (4,), (4,))
    total(7)
    ends_in(1)
    layers((0, 1, 2), (0, 1), (0,))
    sides_in(6)
    layer0(6)
    layer0(7, True)
    conv1(2, (1,))
    conv1(3, (1,))
    for i in (1, 2, 3):
        conv2(i, (2,))

    def drain(ref, sem):
        pltpu.make_async_copy(ref, ref, sem).wait()

    drain(gath.at[:, pl.ds(0, G - 1)], ag_send)
    drain(send1.at[:, :, pl.ds(0, B * (CHUNK - ROWS))], a1_send)
    drain(send2.at[:, :, pl.ds(0, B * (CHUNK - ROWS))], a2_send)
    drain(part.at[:, pl.ds(0, G - 1)], rs_send)
    for dz, dx in near:
        for p in range(1 if dz else B):
            halo(dz, dx, p).wait_send()
    sides_in(7)
    layer0(7)
    conv1(2, (0, 2))
    conv1(3, (0, 2))
    for i in (1, 2, 3):
        conv2(i, (0, 1, 3, 4))
    for i in (1, 2, 3):
        conv3(i)
    for z in range(B):
        last(z)


def body(estimate, coil_maps, measured, line_mask, w_first, w_middle, w_last):
    tabs = [jnp.asarray(t) for t in tables()]
    measured = measured.reshape(2, 2, N * B, N)
    w_first = jnp.transpose(w_first, (0, 2, 1))
    operands = (estimate, coil_maps, measured, line_mask, w_first, w_middle, w_last, *tabs)
    vmem = pl.BlockSpec(memory_space=pltpu.VMEM)
    dma = pltpu.SemaphoreType.DMA
    block = pltpu.VMEM((2, B, B, N), F32)
    return pl.pallas_call(
        kernel,
        out_shape=(block, block),
        in_specs=[pl.BlockSpec(memory_space=pl.ANY)] * len(operands),
        out_specs=(vmem, vmem),
        scratch_shapes=[pltpu.VMEM(a.shape, a.dtype) for a in (
            estimate, coil_maps, measured, line_mask, w_first, w_middle, w_last,
            tabs[0], tabs[1], tabs[2], tabs[3], tabs[4], tabs[5])] + [
            pltpu.VMEM((B, G, 2, B, N), F32),
            pltpu.VMEM((2, 2, N * B, N), F32),
            pltpu.VMEM((2, 2, N * B, N), F32),
            pltpu.VMEM((2, 2, N * B, N), F32),
            pltpu.VMEM((2, 2, N * B, N), F32),
            pltpu.VMEM((B, G, 2, B, N), F32),
            pltpu.VMEM((B, G, 2, B, N), F32),
            pltpu.VMEM((1152, 512), BF16),
            pltpu.VMEM((192, 1152), BF16),
            pltpu.VMEM((288, 384), BF16),
            pltpu.VMEM((3, 2, 14, B, N), F32),
            pltpu.VMEM((48, 14 * N), BF16), pltpu.VMEM((48, 14 * N), BF16),
            pltpu.VMEM((384, 12 * N), BF16), pltpu.VMEM((384, 12 * N), BF16),
            pltpu.VMEM((320, 10 * N), BF16), pltpu.VMEM((320, 10 * N), BF16),
            pltpu.VMEM((10, 144, N), F32),
            dma((13,)), dma, dma((B,)), dma, dma((2, B)), dma, dma((2, B)), dma, dma((B,)), dma((22,)), dma((22,)),
        ],
        compiler_params=pltpu.CompilerParams(
            collective_id=0, has_side_effects=True, vmem_limit_bytes=56 * 2**20),
    )(*operands)


def solution(mesh):
    in_specs = (
        P(None, "slab", "coil", None),
        P("coil", None, "slab", None, None),
        P("coil", None, None, "slab", None),
        P(),
        P(),
        P(),
        P(),
    )
    out_specs = (P(None, "slab", "coil", None), P(None, "slab", "coil", None))
    return jax.shard_map(body, mesh=mesh, in_specs=in_specs, out_specs=out_specs, check_vma=False)
```

```python
import math

import jax
import jax.numpy as jnp
import ml_dtypes
import numpy as np
from jax import lax
from jax.experimental import pallas as pl
from jax.experimental.pallas import tpu as pltpu
from jax.sharding import PartitionSpec as P

MESH = pl.DeviceIdType.MESH
F32 = jnp.float32
BF16 = jnp.bfloat16
N = 128
B = 8
G = 16
ROWS = B
CHUNK = G * ROWS


def tables():
    k = np.arange(N)
    angle = 2.0 * math.pi * (np.outer(k, k) % N) / N
    c, s = np.cos(angle) / math.sqrt(N), np.sin(angle) / math.sqrt(N)
    fwd = np.block([[c, s], [-s, c]])
    inv = np.block([[c, -s], [s, c]])

    def pieces(m):
        hi = m.astype(np.float32).astype(ml_dtypes.bfloat16)
        lo = (m - hi.astype(np.float64)).astype(np.float32).astype(ml_dtypes.bfloat16)
        return [hi, hi, lo]

    order = np.arange(N).reshape(G, B).T.reshape(-1)
    order = np.concatenate([order, order + N])
    return [
        np.concatenate(pieces(fwd), 1),
        np.concatenate(pieces(inv), 1),
        np.concatenate(pieces(inv), 0),
        np.concatenate(pieces(fwd), 0),
        np.concatenate(pieces(fwd[:, order]), 1),
        np.concatenate(pieces(inv[order]), 1),
    ]


def split(x):
    hi = x.astype(BF16)
    lo = (x - hi.astype(F32)).astype(BF16)
    return hi, lo


def left(table, x):
    hi, lo = split(x)
    return jnp.dot(table, jnp.concatenate([hi, lo, hi], 0), preferred_element_type=F32)


def right(x, table):
    hi, lo = split(x)
    return jnp.dot(jnp.concatenate([hi, lo, hi], 1), table, preferred_element_type=F32)


def loop(count, fn):
    def step(i, carry):
        fn(i)
        return carry

    lax.fori_loop(0, count, step, 0)


def shifted_sum(p0, p1, p2):
    lane = lax.broadcasted_iota(jnp.int32, p0.shape, 1)
    down = jnp.where(lane == 0, 0.0, pltpu.roll(p0, 1, 1))
    up = jnp.where(lane == N - 1, 0.0, pltpu.roll(p2, N - 1, 1))
    return p1 + down + up


def build_weights(wf, wm, wl, w1, w2, w3):
    lane = lax.broadcasted_iota(jnp.int32, (32, 512), 1)
    for dy in range(3):
        base = jnp.zeros((32, 512), F32)
        for dz in range(3):
            for dx in range(3):
                taps = jnp.transpose(jnp.concatenate([wf[dz * 9 + dx * 3 + dy], jnp.zeros((6, 32), F32)], 0))
                for c in range(2):
                    base = jnp.where(lane == dz * 48 + c * 24 + dx + 5, taps[:, c:c + 1], base)
        hi = base.astype(BF16).astype(F32)
        full = hi + pltpu.roll(hi, 144, 1) + pltpu.roll(base - hi, 288, 1)
        for xo in range(12):
            r = xo // 4 * 384 + dy * 128 + xo % 4 * 32
            w1[r:r + 32, :] = (pltpu.roll(full, xo, 1) if xo else full).astype(BF16)
    for dz in range(3):
        for dy in range(3):
            base = jnp.concatenate(
                [wm[dz * 9 + dx * 3 + dy] for dx in range(3)] + [jnp.zeros((32, 32), F32)], 1)
            for xo in range(2):
                hi, lo = split(pltpu.roll(base, 32, 1) if xo else base)
                r = (dy * 2 + xo) * 32
                for part, value in enumerate((hi, hi, lo)):
                    w2[r:r + 32, part * 384 + dz * 128:part * 384 + dz * 128 + 128] = value
    for dz in range(3):
        for dy in range(3):
            base = jnp.concatenate(
                [wl[dz * 9 + dx * 3 + dy] for dx in range(3)] + [jnp.zeros((2, 416), F32)], 1)
            both = jnp.concatenate([jnp.broadcast_to(base[o:o + 1], (8, 512)) for o in range(2)], 0)
            row = lax.broadcasted_iota(jnp.int32, (16, 512), 0) % 8
            moved = both
            for xo in range(1, 8):
                moved = jnp.where(row == xo, pltpu.roll(both, 32 * xo, 1), moved)
            hi, lo = split(moved[:, :384])
            r = dz * 48 + dy * 16
            w3[r:r + 16, :] = hi
            w3[144 + r:160 + r, :] = lo


def kernel(
    est_in, maps_in, meas_in, mask_in, wf_in, wm_in, wl_in, t0, t1, t2, t3, t4, t5,
    combined, refined,
    est, maps, meas, mask, wf, wm, wl, lf, li, rf, ri_, lzf, lzi,
    gath, send1, recv1, send2, recv2, part, sums,
    w1, w2, w3, big, f0h, f0l, f1h, f1l, f2h, f2l, q3,
    go, load_sem, ag_send, ag_recv, a1_send, a1_recv, a2_send, a2_recv,
    rs_send, rs_recv, halo_send, halo_recv,
):
    me_c = lax.axis_index("coil")
    me_s = lax.axis_index("slab")

    def plane(p):
        return p // 2 + p % 2 * (B - 1 - p // 2 * 2)

    barrier = pltpu.get_barrier_semaphore()

    def near_id(dz, dx):
        return {"coil": lax.rem(me_c + dx + G, G), "slab": lax.rem(me_s + dz + G, G)}

    def far_first(k):
        return lax.rem(me_c + G // 2 + (k + 1) // 2 * (2 * lax.rem(k, 2) - 1) + G, G)

    def greet(sem, target):
        pl.semaphore_signal(sem, inc=1, device_id=target, device_id_type=MESH)

    core = lax.rem(me_c, 2)
    chip = me_c // 2
    sibling = {"coil": me_c + 1 - 2 * core}
    loop(G - 1, lambda k: greet(barrier, {"coil": 2 * chip + 1, "slab": lax.rem(me_s + k + 1, G)}))
    loop(7, lambda k: greet(barrier, {"coil": 2 * lax.rem(chip + k + 1, 8)}))

    @pl.when(core == 1)
    def _():
        greet(barrier, sibling)

    pairs = [(est_in, est), (t0, lf), (maps_in, maps), (wf_in, wf), (wm_in, wm), (wl_in, wl), (t2, rf), (t4, lzf),
             (meas_in, meas), (mask_in, mask), (t5, lzi), (t3, ri_), (t1, li)]
    loads = [pltpu.make_async_copy(a, b, load_sem.at[i]) for i, (a, b) in enumerate(pairs)]
    for load in loads:
        load.start()

    @pl.when(core == 0)
    def _():
        pl.semaphore_wait(barrier, G - 1)
        greet(go, sibling)

    @pl.when(core == 1)
    def _():
        pl.semaphore_wait(go, 1)

    def slabs_ready():
        @pl.when(core == 1)
        def _():
            pl.semaphore_wait(barrier, 2 * (G - 1))
            greet(go, sibling)

        @pl.when(core == 0)
        def _():
            pl.semaphore_wait(go, 1)


    def gather_out(q):
        def out(k):
            pltpu.make_async_remote_copy(
                src_ref=est.at[:, q], dst_ref=gath.at[q, me_c], send_sem=ag_send, recv_sem=ag_recv.at[q],
                device_id={"coil": far_first(k)}, device_id_type=MESH).start()

        loop(G - 1, out)
        gath[q, me_c] = est[:, q]

    def gather_in(q):
        ref = gath.at[q, pl.ds(0, G - 1)]
        pltpu.make_async_copy(ref, ref, ag_recv.at[q]).wait()

    def exchange(buf, dst, c, q, peer, send_sem, recv_sem, turned):
        at = plane(q) if turned else q
        return pltpu.make_async_remote_copy(
            src_ref=buf.at[c, :, pl.ds(pl.multiple_of(at * CHUNK + peer * ROWS, ROWS), ROWS), :],
            dst_ref=dst.at[c, :, pl.ds(pl.multiple_of(at * CHUNK + me_s * ROWS, ROWS), ROWS), :],
            send_sem=send_sem, recv_sem=recv_sem.at[c, q],
            device_id={"slab": peer}, device_id_type=MESH)

    def exchange_out(buf, dst, c, q, send_sem, recv_sem, turned=False):
        def out(k):
            exchange(buf, dst, c, q, lax.rem(me_s + k + 1, G), send_sem, recv_sem, turned).start()

        loop(G - 1, out)
        at = plane(q) if turned else q
        own = pl.ds(pl.multiple_of(at * CHUNK + me_s * ROWS, ROWS), ROWS)
        for r in range(2):
            dst[c, r, own, :] = buf[c, r, own, :]

    def all_of(buf, c, q):
        return buf.at[c, :, pl.ds(pl.multiple_of(q * CHUNK, CHUNK), CHUNK - ROWS), :]

    def exchange_in(dst, c, q, recv_sem):
        ref = all_of(dst, c, q)
        pltpu.make_async_copy(ref, ref, recv_sem.at[c, q]).wait()

    def slab_plane(c, q, first=False):
        ir = gath[q, :, 0].reshape(N, N)
        ii = gath[q, :, 1].reshape(N, N)
        mr = maps[c, 0, q]
        mi = maps[c, 1, q]
        y = left(lf[...], jnp.concatenate([mr * ir - mi * ii, mr * ii + mi * ir], 0))
        for r in range(2):
            send1[c, r, pl.ds(pl.multiple_of(q * CHUNK, CHUNK), CHUNK), :] = y[r * N:(r + 1) * N]
        if first:
            slabs_ready()
        exchange_out(send1, recv1, c, q, a1_send, a1_recv)

    loads[0].wait()
    for q in range(3):
        gather_out(q)
    loads[1].wait()
    loads[2].wait()
    for q in range(B):
        gather_in(q)
        if q + 3 < B:
            gather_out(q + 3)
        slab_plane(0, q, q == 0)
        if q < 2:
            slab_plane(1, q)
    loop(B - 2, lambda q: slab_plane(1, q + 2))

    for load in loads[3:]:
        load.wait()
    build_weights(wf, wm, wl, w1, w2, w3)

    def pencils(c):
        loop(B, lambda q: exchange_in(recv1, c, q, a1_recv))

        def pair(kp):
            rows = []
            for j in range(2):
                rows.append(jnp.concatenate(
                    [recv1[c, r, pl.ds(2 * kp + j, N, stride=ROWS), :] for r in range(2)], 1))
            y = right(jnp.concatenate(rows, 0), rf[...])
            x = jnp.concatenate([
                jnp.concatenate([y[:N, :N], y[N:, :N]], 1),
                jnp.concatenate([y[:N, N:], y[N:, N:]], 1)], 0)
            x = left(lzf[...], x)
            w = jnp.where(mask[...] == 1, 0.5, 0.0)
            halves = []
            for r in range(2):
                pieces = []
                for j in range(2):
                    k = x[r * N:(r + 1) * N, j * N:(j + 1) * N]
                    m = meas[c, r, pl.ds(2 * kp + j, N, stride=B), :]
                    pieces.append(k - w * (k - m))
                halves.append(jnp.concatenate(pieces, 1))
            x = left(lzi[...], jnp.concatenate(halves, 0))
            y = jnp.concatenate([
                jnp.concatenate([x[:N, :N], x[N:, :N]], 1),
                jnp.concatenate([x[:N, N:], x[N:, N:]], 1)], 0)
            y = right(y, ri_[...])
            for j in range(2):
                for r in range(2):
                    send2[c, r, pl.ds(2 * kp + j, N, stride=ROWS), :] = y[j * N:(j + 1) * N, r * N:(r + 1) * N]

        loop(4, pair)
        loop(B, lambda p: exchange_out(send2, recv2, c, p, a2_send, a2_recv, True))

    loop(2, pencils)

    def coil_back(c, p):
        exchange_in(recv2, c, p, a2_recv)
        z = plane(p)
        at = pl.ds(pl.multiple_of(z * CHUNK, CHUNK), CHUNK)
        x = left(li[...], jnp.concatenate([recv2[c, 0, at, :], recv2[c, 1, at, :]], 0))
        br = x[:N]
        bi = x[N:]
        mr = maps[c, 0, z]
        mi = maps[c, 1, z]
        for r, v in enumerate((mr * br + mi * bi, mr * bi - mi * br)):
            v = v.reshape(G, B, N)
            part[p, :, r] = v if c == 0 else part[p, :, r] + v

    near = [(a, b) for a in (-1, 0, 1) for b in (-1, 0, 1) if (a, b) != (0, 0)]

    def halo(dz, dx, p=0):
        if dz:
            a, b, n = (3, 11, 3) if dz < 0 else (8, 0, 3)
            i = dx + 1 + 3 * (dz > 0)
        else:
            a, b, n = 3 + plane(p), 3 + plane(p), 1
            i = 6 + 2 * p + (dx + 1) // 2
        return pltpu.make_async_remote_copy(
            src_ref=big.at[1, :, pl.ds(a, n)], dst_ref=big.at[1 - dx, :, pl.ds(b, n)],
            send_sem=halo_send.at[i], recv_sem=halo_recv.at[i],
            device_id=near_id(dz, dx), device_id_type=MESH)

    def spread(p):
        def out(k):
            target = far_first(k)
            pltpu.make_async_remote_copy(
                src_ref=part.at[p, target], dst_ref=sums.at[p, me_c], send_sem=rs_send, recv_sem=rs_recv.at[p],
                device_id={"coil": target}, device_id_type=MESH).start()

        loop(G - 1, out)
        sums[p, me_c] = part[p, me_c]

    def total(p):
        ref = sums.at[p, pl.ds(0, G - 1)]
        pltpu.make_async_copy(ref, ref, rs_recv.at[p]).wait()
        value = sums[p, 0]
        for k in range(1, G):
            value = value + sums[p, k]
        big[1, :, 3 + plane(p)] = value
        halo(0, -1, p).start()
        halo(0, 1, p).start()
        if p in (4, 5):
            for dx in (0, -1, 1):
                halo(2 * p - 9, dx).start()
        combined[:, plane(p)] = value

    low_c, high_c, low_s, high_s = me_c == 0, me_c == G - 1, me_s == 0, me_s == G - 1

    def guard(v, *outside):
        for out, here in outside:
            if here:
                v = jnp.where(out, 0.0, v)
        return v

    def layer0(z, alone=False):
        rows = []
        for c in range(2):
            for blk in range(3):
                if alone and blk != 1:
                    rows.append(jnp.zeros((B, N), F32))
                    continue
                rows.append(guard(
                    big[blk, c, z], (low_c, blk == 0), (high_c, blk == 2), (low_s, z < 3), (high_s, z >= 11)))
        f0h[:, z * N:(z + 1) * N], f0l[:, z * N:(z + 1) * N] = split(jnp.concatenate(rows, 0))

    def window(hi, lo, i, rows):
        h = [hi[rows, (2 * i + dz) * N:(2 * i + dz + 2) * N] for dz in range(3)]
        l = [lo[rows, (2 * i + dz) * N:(2 * i + dz + 2) * N] for dz in range(3)]
        return jnp.concatenate(h + l + h, 0)

    def conv1(i, groups=(0, 1, 2)):
        data = window(f0h, f0l, i, slice(0, 48))
        for g in groups:
            y = jnp.dot(w1[g * 384:(g + 1) * 384, 0:432], data, preferred_element_type=F32)
            for j in range(2):
                z = 2 * i + j
                v = jnp.maximum(shifted_sum(*[y[d * 128:(d + 1) * 128, j * N:(j + 1) * N] for d in range(3)]), 0.0)
                v = guard(v, (low_s, z < 2), (high_s, z >= 10))
                v = jnp.concatenate([
                    guard(v[:64], (low_c, g == 0)), guard(v[64:], (high_c, g == 2))], 0)
                at = (slice(g * 128, (g + 1) * 128), slice(z * N, (z + 1) * N))
                f1h[at], f1l[at] = split(v)

    def conv2(i, groups=(0, 1, 2, 3, 4)):
        for g in groups:
            data = window(f1h, f1l, i, slice(g * 64, g * 64 + 128))
            y = jnp.dot(w2[...], data, preferred_element_type=F32)
            for j in range(2):
                z = 2 * i + j
                v = jnp.maximum(shifted_sum(*[y[d * 64:(d + 1) * 64, j * N:(j + 1) * N] for d in range(3)]), 0.0)
                v = guard(v, (low_s, z < 1), (high_s, z >= 9))
                v = jnp.concatenate([
                    guard(v[:32], (low_c, g == 0)), guard(v[32:], (high_c, g == 4))], 0)
                at = (slice(g * 64, (g + 1) * 64), slice(z * N, (z + 1) * N))
                f2h[at], f2l[at] = split(v)

    def conv3(i):
        at = slice(2 * i * N, (2 * i + 2) * N)
        y = jnp.dot(w3[:, 0:320], f2h[:, at], preferred_element_type=F32)
        y = y[:144] + y[144:] + jnp.dot(w3[0:144, 0:320], f2l[:, at], preferred_element_type=F32)
        q3[2 * i] = y[:, :N]
        q3[2 * i + 1] = y[:, N:]

    def sides_in(*quarters):
        for p in quarters:
            halo(0, -1, p).wait_recv()
            halo(0, 1, p).wait_recv()

    def ends_in(dz):
        for dx in (-1, 0, 1):
            halo(dz, dx).wait_recv()

    def layers(planes, firsts, seconds):
        for z in planes:
            layer0(z)
        for i in firsts:
            conv1(i)
        for i in seconds:
            conv2(i)
        for i in seconds:
            conv3(i)

    def last(z):
        p = []
        for dy in range(3):
            p.append(sum(q3[z + dz, dz * 48 + dy * 16:dz * 48 + dy * 16 + 16, :] for dz in range(3)))
        v = shifted_sum(*p)
        for c in range(2):
            refined[c, z] = big[1, c, 3 + z] + v[c * B:(c + 1) * B]

    loop(B, lambda p: coil_back(0, p))
    for p in range(B):
        coil_back(1, p)
        spread(p)
        if p > 1:
            total(p - 2)
    sides_in(0, 1, 2, 3, 4)
    ends_in(-1)
    layers((3, 4, 5, 9, 10, 11, 12, 13), (5,), ())
    total(6)
    sides_in(5)
    layers((8,), (4,), (4,))
    total(7)
    ends_in(1)
    layers((0, 1, 2), (0, 1), (0,))
    sides_in(6)
    layer0(6)
    layer0(7, True)
    conv1(2, (1,))
    conv1(3, (1,))
    for i in (1, 2, 3):
        conv2(i, (2,))

    def drain(ref, sem):
        pltpu.make_async_copy(ref, ref, sem).wait()

    drain(gath.at[:, pl.ds(0, G - 1)], ag_send)
    drain(send1.at[:, :, pl.ds(0, B * (CHUNK - ROWS))], a1_send)
    drain(send2.at[:, :, pl.ds(0, B * (CHUNK - ROWS))], a2_send)
    drain(part.at[:, pl.ds(0, G - 1)], rs_send)
    for dz, dx in near:
        for p in range(1 if dz else B):
            halo(dz, dx, p).wait_send()
    sides_in(7)
    layer0(7)
    conv1(2, (0, 2))
    conv1(3, (0, 2))
    for i in (1, 2, 3):
        conv2(i, (0, 1, 3, 4))
    for i in (1, 2, 3):
        conv3(i)
    for z in range(B):
        last(z)


def body(estimate, coil_maps, measured, line_mask, w_first, w_middle, w_last):
    tabs = [jnp.asarray(t) for t in tables()]
    measured = measured.reshape(2, 2, N * B, N)
    w_first = jnp.transpose(w_first, (0, 2, 1))
    operands = (estimate, coil_maps, measured, line_mask, w_first, w_middle, w_last, *tabs)
    vmem = pl.BlockSpec(memory_space=pltpu.VMEM)
    dma = pltpu.SemaphoreType.DMA
    block = pltpu.VMEM((2, B, B, N), F32)
    return pl.pallas_call(
        kernel,
        out_shape=(block, block),
        in_specs=[pl.BlockSpec(memory_space=pl.ANY)] * len(operands),
        out_specs=(vmem, vmem),
        scratch_shapes=[pltpu.VMEM(a.shape, a.dtype) for a in (
            estimate, coil_maps, measured, line_mask, w_first, w_middle, w_last,
            tabs[0], tabs[1], tabs[2], tabs[3], tabs[4], tabs[5])] + [
            pltpu.VMEM((B, G, 2, B, N), F32),
            pltpu.VMEM((2, 2, N * B, N), F32),
            pltpu.VMEM((2, 2, N * B, N), F32),
            pltpu.VMEM((2, 2, N * B, N), F32),
            pltpu.VMEM((2, 2, N * B, N), F32),
            pltpu.VMEM((B, G, 2, B, N), F32),
            pltpu.VMEM((B, G, 2, B, N), F32),
            pltpu.VMEM((1152, 512), BF16),
            pltpu.VMEM((192, 1152), BF16),
            pltpu.VMEM((288, 384), BF16),
            pltpu.VMEM((3, 2, 14, B, N), F32),
            pltpu.VMEM((48, 14 * N), BF16), pltpu.VMEM((48, 14 * N), BF16),
            pltpu.VMEM((384, 12 * N), BF16), pltpu.VMEM((384, 12 * N), BF16),
            pltpu.VMEM((320, 10 * N), BF16), pltpu.VMEM((320, 10 * N), BF16),
            pltpu.VMEM((10, 144, N), F32),
            pltpu.SemaphoreType.REGULAR, dma((13,)), dma, dma((B,)), dma, dma((2, B)), dma, dma((2, B)), dma, dma((B,)), dma((22,)), dma((22,)),
        ],
        compiler_params=pltpu.CompilerParams(
            collective_id=0, has_side_effects=True, vmem_limit_bytes=56 * 2**20),
    )(*operands)


def solution(mesh):
    in_specs = (
        P(None, "slab", "coil", None),
        P("coil", None, "slab", None, None),
        P("coil", None, None, "slab", None),
        P(),
        P(),
        P(),
        P(),
    )
    out_specs = (P(None, "slab", "coil", None), P(None, "slab", "coil", None))
    return jax.shard_map(body, mesh=mesh, in_specs=in_specs, out_specs=out_specs, check_vma=False)
```
